32 devices in a mesh: seq: 8 (over y, x, core), head: 4 (over z).
Axes of the slice: x: 2, y: 2, z: 4, core: 2. Of those that a mesh axis runs over, the one named last changes fastest.
Arguments:
- queries: float32 [4096, 1024], P('seq', 'head'), may hold values from -6 to 6
- keys: float32 [4096, 1024], P('seq', 'head'), may hold values from -6 to 6
- values: float32 [4096, 1024], P('seq', 'head'), may hold values from -60 to 60
- cotangent: float32 [4096, 1024], P('seq', 'head'), may hold values from -6 to 6
- gain: float32 [1024], P('head'), may hold values from 0.1 to 1.9
Outputs:
- grad_queries: float32 [4096, 1024], P('seq', 'head')
- grad_keys: float32 [4096, 1024], P('seq', 'head')
- grad_values: float32 [4096, 1024], P('seq', 'head')
The draws below stay inside these ranges and needn't reach their ends.
All inputs are finite; a program needn't handle non-finite values.
Results may differ from the reference program's by a relative error of at most 0.0001.
Values sent between devices are 32-bit elements; how exact they have to be, the bound alone decides.
No kernel may reach another device: no remote copies, remote signals or barrier semaphores. Data moves between devices by JAX's collectives and lax.ppermute only.
A program may use at most 64 MiB of HBM per device.

```python
import math
import jax
import jax.numpy as jnp
from jax import lax

HD = 128
HEADS = 8
D = 1024
TOKENS = 4096


def draw_values(key, part):
    key_spread = jax.random.fold_in(key, 11)
    key_noise = jax.random.fold_in(key, 12)
    head_index = jnp.arange(HEADS).astype(jnp.float32)
    rising = 3.0 ** (head_index / (HEADS - 1))
    spreads = jnp.exp(jax.random.uniform(key_spread, (HEADS,), minval=0.0, maxval=math.log(3.5)))
    head_scale = jnp.repeat(rising * spreads, HD)
    noise_field = jnp.clip(jax.random.normal(key_noise, (TOKENS, D)), -5.0, 5.0)
    return (noise_field * head_scale[None, :]).astype(jnp.float32)


def block_scale(rng, dims, shards, least, largest):
    def one(position, blocks):
        steps = jax.random.uniform(jax.random.fold_in(jax.random.fold_in(rng, 6), position), (blocks,), jnp.float32, least / len(shards), largest / len(shards))
        return jnp.repeat(jnp.exp(steps), dims[position] // blocks).reshape((-1,) + (1,) * (len(dims) - position - 1))

    factor_of = one(*shards[0])
    for cut in shards[1:]:
        factor_of = factor_of * one(*cut)
    return factor_of


def noise(key, dims, scale, reach, shards=(), dtype=jnp.bfloat16):
    result = jax.random.normal(key, dims, jnp.float32) * scale
    if len(shards) > 0:
        result = block_scale(key, dims, shards, -0.22, 0.18) * result
    return jnp.clip(result, min=-reach, max=reach).astype(dtype)


def setup_inputs(seed: int = 0) -> dict:
    streams_of = jax.random.split(jax.random.key(seed), 6)
    return {
        "queries": noise(streams_of[0], (TOKENS, D), 1.0, 6.0, ((0, 8), (1, 4)), jnp.float32),
        "keys": noise(streams_of[1], (TOKENS, D), 1.0, 6.0, ((0, 8), (1, 4)), jnp.float32),
        "values": draw_values(jax.random.fold_in(streams_of[5], 71), 0),
        "cotangent": noise(streams_of[3], (TOKENS, D), 1.0, 6.0, ((0, 8), (1, 4)), jnp.float32),
        "gain": jnp.clip(1.0 + 0.18 * jax.random.normal(streams_of[4], (D,), jnp.float32), 0.1, 1.9),
    }


def product(form, left, right):
    return jnp.einsum(form, left, right, precision=lax.Precision.HIGHEST)

def to_blocks(array, block):
    return array.reshape(TOKENS // block, block, HEADS, HD).transpose(0, 2, 1, 3)

def from_blocks(array):
    return array.transpose(0, 2, 1, 3).reshape(TOKENS, HEADS * HD)

def reference(queries, keys, values, cotangent, gain):
    block = min(512, TOKENS)
    query_blocks = to_blocks(queries, block)
    key_blocks = to_blocks(keys, block)
    value_blocks = to_blocks(values, block)
    causal = (jnp.arange(block)[:, None] >= jnp.arange(block)[None, :]).astype(jnp.float32)

    def forward_step(state, inputs):
        query_now, key_now, value_now = inputs
        scores = product('htd,hsd->hts', query_now, key_now) * causal
        attended = product('hts,hse->hte', scores, value_now) + product('htd,hde->hte', query_now, state)
        new_state = state + product('hsd,hse->hde', key_now, value_now)
        return (new_state, (attended, state))
    start_state = jnp.zeros((HEADS, HD, HD), jnp.float32)
    unused_state, (attended_blocks, state_before) = lax.scan(forward_step, start_state, (query_blocks, key_blocks, value_blocks))
    attended_rows = from_blocks(attended_blocks)
    scaled_cot = gain[None, :] * cotangent
    inverse = lax.rsqrt(lax.optimization_barrier(jnp.mean(attended_rows * attended_rows, axis=1)) + 1e-06)
    cross = lax.optimization_barrier(jnp.mean(scaled_cot * attended_rows, axis=1))
    grad_rows = inverse[:, None] * scaled_cot - attended_rows * (inverse * inverse * inverse * cross)[:, None]
    grad_blocks = to_blocks(grad_rows, block)

    def backward_step(state_after, inputs):
        query_now, key_now, value_now, grad_now, before_now = inputs
        scores = product('htd,hsd->hts', query_now, key_now) * causal
        mixing = product('hte,hse->hts', grad_now, value_now) * causal
        grad_q = product('hts,hsd->htd', mixing, key_now) + product('hde,hte->htd', before_now, grad_now)
        grad_k = product('hts,htd->hsd', mixing, query_now) + product('hde,hse->hsd', state_after, value_now)
        grad_v = product('hts,hte->hse', scores, grad_now) + product('hde,hsd->hse', state_after, key_now)
        new_after = state_after + product('htd,hte->hde', query_now, grad_now)
        return (new_after, (grad_q, grad_k, grad_v))
    unused_after, (grad_q, grad_k, grad_v) = lax.scan(backward_step, start_state, (query_blocks, key_blocks, value_blocks, grad_blocks, state_before), reverse=True)
    return (from_blocks(grad_q), from_blocks(grad_k), from_blocks(grad_v))
```

```python
import functools
import jax
import jax.numpy as jnp
from jax import lax
from jax.experimental import pallas as pl
from jax.experimental.pallas import tpu as pltpu
from jax.sharding import PartitionSpec as P

HD = 128
BLOCK = 256
LANES = 128
F32 = jnp.float32
BF16 = jnp.bfloat16
NN = ((1,), (0,))
NT = ((1,), (1,))
TN = ((0,), (0,))


def split(x):
    high = x.astype(BF16)
    return high, (x - high.astype(F32)).astype(BF16)


def mul(left, right, dims):
    return lax.dot_general(left, right, (dims, ((), ())), preferred_element_type=F32)


def product(left, right, dims):
    return (
        mul(left[0], right[0], dims)
        + mul(left[0], right[1], dims)
        + mul(left[1], right[0], dims)
    )


def heads(width):
    return [slice(h * HD, (h + 1) * HD) for h in range(width // HD)]


def blocks(rows):
    size = min(BLOCK, rows)
    return [slice(n * size, (n + 1) * size) for n in range(rows // size)]


def call(body, name, out_shape, flops, *operands):
    out_shape = [jax.ShapeDtypeStruct(shape, F32) for shape in out_shape]
    moved = 4 * sum(x.size for x in list(operands) + out_shape)
    return pl.pallas_call(
        body,
        out_shape=out_shape,
        name=name,
        cost_estimate=pl.CostEstimate(flops=flops, bytes_accessed=moved, transcendentals=0),
        compiler_params=pltpu.CompilerParams(vmem_limit_bytes=16 * 1024 * 1024),
    )(*operands)


def by_core(core, first, second):
    return jnp.where(core == 0, first, second)


def store_halves(core, total, mine_ref, other_ref):
    half = total.shape[0] // 2
    mine_ref[...] = by_core(core, total[:half], total[half:])
    other_ref[...] = by_core(core, total[half:], total[:half])


def key_states(core_ref, k_ref, v_ref, mine_ref, other_ref, before_ref):
    rows, width = k_ref.shape
    states = []
    for col in heads(width):
        total = None
        for n, row in enumerate(blocks(rows)):
            state = product(split(k_ref[row, col]), split(v_ref[row, col]), TN)
            total = state if total is None else total + state
            if n + 1 < len(blocks(rows)):
                before_ref[n, col, :] = total
        states.append(total)
    store_halves(core_ref[0, 0], jnp.concatenate(states, axis=0), mine_ref, other_ref)


def causal_mask(size, transposed=False):
    row = lax.broadcasted_iota(jnp.int32, (size, size), 0)
    col = lax.broadcasted_iota(jnp.int32, (size, size), 1)
    return row <= col if transposed else row >= col


def attend_local(q_ref, k_ref, v_ref, out_ref):
    rows, width = q_ref.shape
    for col in heads(width):
        for row in blocks(rows):
            scores = product(split(q_ref[row, col]), split(k_ref[row, col]), NT)
            scores = jnp.where(causal_mask(scores.shape[0]), scores, 0.0)
            out_ref[row, col] = product(split(scores), split(v_ref[row, col]), NN)


def incoming(core, keep, got, col):
    half = keep.shape[0]
    if col.start < half:
        return by_core(core, keep[col], got[col])
    col = slice(col.start - half, col.stop - half)
    return by_core(core, got[col], keep[col])


def attend_state(core_ref, q_ref, local_ref, cot_ref, gain_ref, keep_ref, got_ref, before_ref, out_ref, sums_ref):
    rows, width = q_ref.shape
    core = core_ref[0, 0]
    for col in heads(width):
        state = incoming(core, keep_ref, got_ref, col)
        for n, row in enumerate(blocks(rows)):
            here = state if n == 0 else state + before_ref[n - 1, col, :]
            out_ref[row, col] = local_ref[row, col] + product(split(q_ref[row, col]), split(here), NN)
    count = rows // LANES
    lane = lax.broadcasted_iota(jnp.int32, (LANES, LANES), 1)
    tile = jnp.zeros((LANES, LANES), F32)
    for j in range(count):
        row = slice(j * LANES, (j + 1) * LANES)
        out = out_ref[row, :]
        squares = jnp.sum(out * out, axis=1, keepdims=True)
        cross = jnp.sum(gain_ref[...] * cot_ref[row, :] * out, axis=1, keepdims=True)
        tile = jnp.where(lane == j, squares, tile)
        tile = jnp.where(lane == count + j, cross, tile)
    sums_ref[...] = tile.T[: 2 * count]


def row_factors(full_width, sums):
    count = sums.shape[0] // 2
    inverse = lax.rsqrt(sums[:count] / full_width + 1e-06)
    factor = inverse * inverse * inverse * (sums[count:] / full_width)
    both = jnp.concatenate([inverse, factor], axis=0)
    tile = jnp.concatenate([both] * (LANES // both.shape[0]), axis=0).T
    return [(tile[:, j : j + 1], tile[:, count + j : count + j + 1]) for j in range(count)]


def grad_of_block(factors, att_ref, cot_ref, gain_ref, row, col):
    parts = []
    for j in range(row.start // LANES, row.stop // LANES):
        part = slice(j * LANES, (j + 1) * LANES)
        inverse, factor = factors[j]
        parts.append(inverse * (gain_ref[:, col] * cot_ref[part, col]) - att_ref[part, col] * factor)
    return jnp.concatenate(parts, axis=0)


def grad_states(full_width, core_ref, sums_ref, q_ref, att_ref, cot_ref, gain_ref, mine_ref, other_ref, after_ref):
    rows, width = q_ref.shape
    factors = row_factors(full_width, sums_ref[...])
    states = []
    for col in heads(width):
        total = None
        for n, row in reversed(list(enumerate(blocks(rows)))):
            grad = grad_of_block(factors, att_ref, cot_ref, gain_ref, row, col)
            state = product(split(q_ref[row, col]), split(grad), TN)
            total = state if total is None else total + state
            if n > 0:
                after_ref[n - 1, col, :] = total
        states.append(total)
    store_halves(core_ref[0, 0], jnp.concatenate(states, axis=0), mine_ref, other_ref)


def grads_local(full_width, core_ref, sums_ref, q_ref, k_ref, v_ref, att_ref, cot_ref, gain_ref, keep_ref, got_ref, before_ref, gq_ref, gk_ref, gv_ref):
    rows, width = q_ref.shape
    core = core_ref[0, 0]
    factors = row_factors(full_width, sums_ref[...])
    for col in heads(width):
        state = incoming(core, keep_ref, got_ref, col)
        for n, row in enumerate(blocks(rows)):
            here = state if n == 0 else state + before_ref[n - 1, col, :]
            grad = split(grad_of_block(factors, att_ref, cot_ref, gain_ref, row, col))
            query, key, value = split(q_ref[row, col]), split(k_ref[row, col]), split(v_ref[row, col])
            size = row.stop - row.start
            lower, upper = causal_mask(size), causal_mask(size, True)
            mixing = jnp.where(lower, product(grad, value, NT), 0.0)
            gq_ref[row, col] = product(split(mixing), key, NN) + product(grad, split(here), NT)
            mixing = jnp.where(upper, product(value, grad, NT), 0.0)
            gk_ref[row, col] = product(split(mixing), query, NN)
            scores = jnp.where(upper, product(key, query, NT), 0.0)
            gv_ref[row, col] = product(split(scores), grad, NN)


def grads_state(core_ref, k_ref, v_ref, gk_local_ref, gv_local_ref, keep_ref, got_ref, after_ref, gk_ref, gv_ref):
    rows, width = k_ref.shape
    core = core_ref[0, 0]
    last = len(blocks(rows)) - 1
    for col in heads(width):
        state = incoming(core, keep_ref, got_ref, col)
        for n, row in enumerate(blocks(rows)):
            here = split(state if n == last else state + after_ref[n, col, :])
            gk_ref[row, col] = gk_local_ref[row, col] + product(split(v_ref[row, col]), here, NT)
            gv_ref[row, col] = gv_local_ref[row, col] + product(split(k_ref[row, col]), here, NN)


def swap(x, axis, distance):
    count = lax.axis_size(axis)
    return lax.ppermute(x, axis, [(i, i ^ distance) for i in range(count)])


def carried(mine, other, reverse):
    place = lax.axis_index("seq")
    core, chip = place % 2, place // 2
    chips = lax.axis_size("seq") // 2
    from_pair = swap(other, "seq", 1)
    pair = mine + from_pair
    total = jnp.zeros_like(pair)
    if chips <= 4:
        got = [(d, swap(pair, "seq", 2 * d)) for d in range(1, chips)]
        for d, part in got:
            ahead = (chip ^ d) > chip if reverse else (chip ^ d) < chip
            total = total + jnp.where(ahead, part, 0.0)
    else:
        d = 1
        while d < chips:
            part = swap(pair, "seq", 2 * d)
            ahead = (chip ^ d) > chip if reverse else (chip ^ d) < chip
            total = total + jnp.where(ahead, part, 0.0)
            pair = pair + part
            d *= 2
    far = 0 if reverse else 1
    keep = total + jnp.where(core == far, from_pair, 0.0)
    give = total + jnp.where(core == far, 0.0, mine)
    return keep, swap(give, "seq", 1)


def sum_over_heads(x):
    count = lax.axis_size("head")
    if count > 4 or count & (count - 1):
        return lax.psum(x, "head")
    return x + sum(swap(x, "head", d) for d in range(1, count))


def shards(queries, keys, values, cotangent, gain):
    rows, width = queries.shape
    full_width = width * lax.axis_size("head")
    count = len(blocks(rows))
    square = rows * width * HD * 2 * 3
    state = (width // 2, HD)
    inner = (max(count - 1, 1), width, HD)
    core = (lax.axis_index("seq") % 2).astype(jnp.int32).reshape(1, 1)
    gain = gain.reshape(1, width)

    mine, other, before = call(key_states, "key_states", [state, state, inner], square, core, keys, values)
    keep, got = carried(mine, other, False)
    local = call(attend_local, "attend_local", [queries.shape], 4 * square, queries, keys, values)[0]
    attended, sums = call(
        attend_state, "attend_state", [queries.shape, (2 * rows // LANES, LANES)], square,
        core, queries, local, cotangent, gain, keep, got, before,
    )
    sums = sum_over_heads(sums)
    mine, other, after = call(
        functools.partial(grad_states, full_width), "grad_states", [state, state, inner], square,
        core, sums, queries, attended, cotangent, gain,
    )
    keep_after, got_after = carried(mine, other, True)
    grad_q, local_k, local_v = call(
        functools.partial(grads_local, full_width), "grads_local", [queries.shape] * 3, 12 * square,
        core, sums, queries, keys, values, attended, cotangent, gain, keep, got, before,
    )
    grad_k, grad_v = call(
        grads_state, "grads_state", [queries.shape] * 2, 2 * square,
        core, keys, values, local_k, local_v, keep_after, got_after, after,
    )
    return grad_q, grad_k, grad_v


def solution(mesh):
    in_specs = (P("seq", "head"), P("seq", "head"), P("seq", "head"), P("seq", "head"), P("head"))
    out_specs = (P("seq", "head"), P("seq", "head"), P("seq", "head"))
    return jax.shard_map(shards, mesh=mesh, in_specs=in_specs, out_specs=out_specs, check_vma=False)
```

```python
import functools
import jax
import jax.numpy as jnp
from jax import lax
from jax.experimental import pallas as pl
from jax.experimental.pallas import tpu as pltpu
from jax.sharding import PartitionSpec as P

HD = 128
BLOCK = 256
LANES = 128
F32 = jnp.float32
BF16 = jnp.bfloat16
NN = ((1,), (0,))
NT = ((1,), (1,))
TN = ((0,), (0,))


def split(x):
    high = x.astype(BF16)
    return high, (x - high.astype(F32)).astype(BF16)


def mul(left, right, dims):
    return lax.dot_general(left, right, (dims, ((), ())), preferred_element_type=F32)


def beside(*parts):
    return jnp.concatenate(parts, axis=1)


def product_nt(left, right):
    return mul(beside(*left), beside(right[0], right[0]), NT) + mul(left[0], right[1], NT)


def product_nn(left, right):
    size = right[0].shape[1]
    wide = mul(left[0], beside(*right), NN)
    return wide[:, :size] + wide[:, size:] + mul(left[1], right[0], NN)


def product_tn(left, right):
    rows, cols = left[0].shape[1], right[0].shape[1]
    wide = mul(beside(*left), beside(*right), TN)
    return wide[:rows, :cols] + wide[:rows, cols:] + wide[rows:, :cols]


def state_operand(state, transposed):
    high, low = split(state)
    if transposed:
        return jnp.concatenate([beside(high, high), beside(low, jnp.zeros_like(low))], axis=0)
    return jnp.concatenate([beside(high, low), beside(high, jnp.zeros_like(low))], axis=0)


def product_state(left, operand, transposed):
    wide = mul(beside(*left), operand, NT if transposed else NN)
    return wide[:, :HD] + wide[:, HD:]


def heads(width):
    return [slice(h * HD, (h + 1) * HD) for h in range(width // HD)]


def blocks(rows):
    size = min(BLOCK, rows)
    return [slice(n * size, (n + 1) * size) for n in range(rows // size)]


def call(body, name, outs, flops, operands, scratch=(), hbm_in=(), hbm_out=()):
    outs = [out if isinstance(out[0], tuple) else (out, F32) for out in outs]
    outs = [
        pltpu.HBM(*out) if i in hbm_out else jax.ShapeDtypeStruct(*out) for i, out in enumerate(outs)
    ]
    moved = sum(x.size * x.dtype.itemsize for x in operands) * 2
    operands = [
        pltpu.with_memory_space_constraint(x, pltpu.HBM) if i in hbm_in else x for i, x in enumerate(operands)
    ]
    place = lambda far: pl.BlockSpec(memory_space=pltpu.HBM if far else pltpu.VMEM)
    return pl.pallas_call(
        body,
        out_shape=outs,
        in_specs=[place(i in hbm_in) for i in range(len(operands))],
        out_specs=[place(i in hbm_out) for i in range(len(outs))],
        scratch_shapes=list(scratch),
        name=name,
        cost_estimate=pl.CostEstimate(flops=flops, bytes_accessed=moved, transcendentals=0),
        compiler_params=pltpu.CompilerParams(vmem_limit_bytes=16 * 1024 * 1024),
    )(*operands)


def on_first_core():
    return lax.axis_index("seq") % 2 == 0


def store_halves(total, mine_ref, other_ref):
    half = total.shape[0] // 2
    first = on_first_core()
    mine_ref[...] = jnp.where(first, total[:half], total[half:])
    other_ref[...] = jnp.where(first, total[half:], total[:half])


def key_states(k_hbm, v_hbm, mine_ref, other_ref, before_ref, k_ref, v_ref, sems):
    rows, width = k_ref.shape
    pieces = sems.shape[1]
    size = rows // pieces
    copies = []
    for p in range(pieces):
        row = pl.ds(p * size, size)
        copies.append([
            pltpu.make_async_copy(far.at[row], near.at[row], sems.at[i, p])
            for i, (far, near) in enumerate(((k_hbm, k_ref), (v_hbm, v_ref)))
        ])
        for copy in copies[p]:
            copy.start()
    states = {}
    for n, row in enumerate(blocks(rows)):
        for p in range(row.start // size, row.stop // size):
            for copy in copies[p]:
                copy.wait()
        for col in heads(width):
            state = product_tn(split(k_ref[row, col]), split(v_ref[row, col]))
            states[col.start] = states[col.start] + state if n > 0 else state
            if n + 1 < len(blocks(rows)):
                before_ref[n, col, :] = states[col.start]
    store_halves(jnp.concatenate([states[col.start] for col in heads(width)], axis=0), mine_ref, other_ref)


def causal_mask(size, transposed=False):
    row = lax.broadcasted_iota(jnp.int32, (size, size), 0)
    col = lax.broadcasted_iota(jnp.int32, (size, size), 1)
    return row <= col if transposed else row >= col


def attend_local(q_ref, k_ref, v_ref, cot_ref, gain_ref, out_ref, scaled_ref):
    rows, width = q_ref.shape
    for col in heads(width):
        for row in blocks(rows):
            scaled_ref[row, col] = gain_ref[:, col] * cot_ref[row, col]
            scores = product_nt(split(q_ref[row, col]), split(k_ref[row, col]))
            scores = jnp.where(causal_mask(scores.shape[0]), scores, 0.0)
            out_ref[row, col] = product_nn(split(scores), split(v_ref[row, col]))


def incoming(keep_ref, got_ref, col):
    half = keep_ref.shape[0]
    first = on_first_core()
    if col.start < half:
        return jnp.where(first, keep_ref[col, :], got_ref[col, :])
    col = slice(col.start - half, col.stop - half)
    return jnp.where(first, got_ref[col, :], keep_ref[col, :])


def attend_state(q_ref, local_ref, scaled_ref, keep_ref, got_ref, before_ref, out_ref, sums_ref):
    rows, width = q_ref.shape
    for col in heads(width):
        state = incoming(keep_ref, got_ref, col)
        for n, row in enumerate(blocks(rows)):
            here = state_operand(state if n == 0 else state + before_ref[n - 1, col, :], False)
            out_ref[row, col] = local_ref[row, col] + product_state(split(q_ref[row, col]), here, False)
    count = rows // LANES
    lane = lax.broadcasted_iota(jnp.int32, (LANES, LANES), 1)
    tile = jnp.zeros((LANES, LANES), F32)
    for j in range(count):
        row = slice(j * LANES, (j + 1) * LANES)
        out = out_ref[row, :]
        squares = jnp.sum(out * out, axis=1, keepdims=True)
        cross = jnp.sum(scaled_ref[row, :] * out, axis=1, keepdims=True)
        tile = jnp.where(lane == j, squares, tile)
        tile = jnp.where(lane == count + j, cross, tile)
    sums_ref[...] = tile.T[: 2 * count]


def row_factors(full_width, sums):
    count = sums.shape[0] // 2
    inverse = lax.rsqrt(sums[:count] / full_width + 1e-06)
    factor = inverse * inverse * inverse * (sums[count:] / full_width)
    both = jnp.concatenate([inverse, factor], axis=0)
    tile = jnp.concatenate([both] * (LANES // both.shape[0]), axis=0).T
    return [(tile[:, j : j + 1], tile[:, count + j : count + j + 1]) for j in range(count)]


def grad_of_block(factors, att_ref, scaled_ref, row, col):
    parts = []
    for j in range(row.start // LANES, row.stop // LANES):
        part = slice(j * LANES, (j + 1) * LANES)
        inverse, factor = factors[j]
        parts.append(inverse * scaled_ref[part, col] - att_ref[part, col] * factor)
    return jnp.concatenate(parts, axis=0)


def grad_states(full_width, sums_ref, q_ref, att_ref, scaled_ref, mine_ref, other_ref, after_ref, high_ref, low_ref):
    rows, width = q_ref.shape
    factors = row_factors(full_width, sums_ref[...])
    states = []
    for col in heads(width):
        total = None
        for n, row in reversed(list(enumerate(blocks(rows)))):
            grad = split(grad_of_block(factors, att_ref, scaled_ref, row, col))
            high_ref[row, col], low_ref[row, col] = grad
            state = product_tn(split(q_ref[row, col]), grad)
            total = state if total is None else total + state
            if n > 0:
                after_ref[n - 1, col, :] = total
        states.append(total)
    store_halves(jnp.concatenate(states, axis=0), mine_ref, other_ref)


def grads_local(grad_high_ref, grad_low_ref, q_ref, k_ref, v_ref, keep_ref, got_ref, before_ref, gq_hbm, gk_ref, gv_ref, gq_ref, sems):
    rows, width = q_ref.shape
    copies = []
    for col in heads(width):
        state = incoming(keep_ref, got_ref, col)
        for n, row in enumerate(blocks(rows)):
            here = state_operand(state if n == 0 else state + before_ref[n - 1, col, :], True)
            grad = grad_high_ref[row, col], grad_low_ref[row, col]
            mixing = product_nt(grad, split(v_ref[row, col]))
            mixing = jnp.where(causal_mask(row.stop - row.start), mixing, 0.0)
            gq_ref[row, col] = product_nn(split(mixing), split(k_ref[row, col])) + product_state(grad, here, True)
            copies.append(pltpu.make_async_copy(gq_ref.at[row, col], gq_hbm.at[row, col], sems.at[len(copies)]))
            copies[-1].start()
    for col in heads(width):
        for row in blocks(rows):
            grad = grad_high_ref[row, col], grad_low_ref[row, col]
            query, key, value = split(q_ref[row, col]), split(k_ref[row, col]), split(v_ref[row, col])
            mask = causal_mask(row.stop - row.start, True)
            mixing = jnp.where(mask, product_nt(value, grad), 0.0)
            gk_ref[row, col] = product_nn(split(mixing), query)
            scores = jnp.where(mask, product_nt(key, query), 0.0)
            gv_ref[row, col] = product_nn(split(scores), grad)
    for copy in copies:
        copy.wait()


def grads_state(k_ref, v_ref, gk_local_ref, gv_local_ref, keep_ref, got_ref, after_ref, gk_hbm, gv_hbm, gk_ref, gv_ref, sems):
    rows, width = k_ref.shape
    last = len(blocks(rows)) - 1
    unit = 0
    copies = []
    for col in heads(width):
        state = incoming(keep_ref, got_ref, col)
        for n, row in enumerate(blocks(rows)):
            here = state if n == last else state + after_ref[n, col, :]
            gk_ref[row, col] = gk_local_ref[row, col] + product_state(split(v_ref[row, col]), state_operand(here, True), True)
            copies.append(pltpu.make_async_copy(gk_ref.at[row, col], gk_hbm.at[row, col], sems.at[0, unit]))
            copies[-1].start()
            gv_ref[row, col] = gv_local_ref[row, col] + product_state(split(k_ref[row, col]), state_operand(here, False), False)
            copies.append(pltpu.make_async_copy(gv_ref.at[row, col], gv_hbm.at[row, col], sems.at[1, unit]))
            copies[-1].start()
            unit += 1
    for copy in copies:
        copy.wait()


def swap(x, axis, distance):
    count = lax.axis_size(axis)
    return lax.ppermute(x, axis, [(i, i ^ distance) for i in range(count)])


def carried(mine, other, reverse):
    place = lax.axis_index("seq")
    core, chip = place % 2, place // 2
    chips = lax.axis_size("seq") // 2
    from_pair = swap(other, "seq", 1)
    pair = mine + from_pair
    total = jnp.zeros_like(pair)
    if chips <= 4:
        got = [(d, swap(pair, "seq", 2 * d)) for d in range(1, chips)]
        for d, part in got:
            ahead = (chip ^ d) > chip if reverse else (chip ^ d) < chip
            total = total + jnp.where(ahead, part, 0.0)
    else:
        d = 1
        while d < chips:
            part = swap(pair, "seq", 2 * d)
            ahead = (chip ^ d) > chip if reverse else (chip ^ d) < chip
            total = total + jnp.where(ahead, part, 0.0)
            pair = pair + part
            d *= 2
    far = 0 if reverse else 1
    keep = total + jnp.where(core == far, from_pair, 0.0)
    give = total + jnp.where(core == far, 0.0, mine)
    return keep, swap(give, "seq", 1)


def sum_of_other_heads(x):
    count = lax.axis_size("head")
    if count > 4 or count & (count - 1):
        return lax.psum(x, "head") - x
    return sum(swap(x, "head", d) for d in range(1, count))


def shards(queries, keys, values, cotangent, gain):
    rows, width = queries.shape
    full_width = width * lax.axis_size("head")
    count = len(blocks(rows))
    units = count * (width // HD)
    size = rows // count
    square = rows * width * HD * 2 * 3
    whole, half = (rows, width), (width // 2, HD)
    inner = (max(count - 1, 1), width, HD)
    pieces = count

    mine, other, before, keys, values = call(
        key_states, "key_states", [half, half, inner, whole, whole], square, [keys, values],
        [pltpu.SemaphoreType.DMA((2, pieces))], hbm_in=(0, 1),
    )
    keep, got = carried(mine, other, False)
    local, scaled = call(
        attend_local, "attend_local", [whole, whole], 4 * square,
        [queries, keys, values, cotangent, gain.reshape(1, width)],
    )
    attended, own_sums = call(
        attend_state, "attend_state", [whole, (2 * rows // LANES, LANES)], square,
        [queries, local, scaled, keep, got, before],
    )
    other_sums = sum_of_other_heads(own_sums)
    sums = own_sums + other_sums
    mine, other, after, grad_high, grad_low = call(
        functools.partial(grad_states, full_width), "grad_states",
        [half, half, inner, (whole, BF16), (whole, BF16)], square,
        [sums, queries, attended, scaled],
    )
    keep_after, got_after = carried(mine, other, True)
    grad_q, local_k, local_v = call(
        grads_local, "grads_local", [whole] * 3, 13 * square,
        [grad_high, grad_low, queries, keys, values, keep, got, before],
        [pltpu.VMEM(whole, F32), pltpu.SemaphoreType.DMA((units,))], hbm_out=(0,),
    )
    grad_k, grad_v = call(
        grads_state, "grads_state", [whole] * 2, 2 * square,
        [keys, values, local_k, local_v, keep_after, got_after, after],
        [pltpu.VMEM(whole, F32), pltpu.VMEM(whole, F32), pltpu.SemaphoreType.DMA((2, units))], hbm_out=(0, 1),
    )
    return grad_q, grad_k, grad_v


def solution(mesh):
    in_specs = (P("seq", "head"), P("seq", "head"), P("seq", "head"), P("seq", "head"), P("head"))
    out_specs = (P("seq", "head"), P("seq", "head"), P("seq", "head"))
    return jax.shard_map(shards, mesh=mesh, in_specs=in_specs, out_specs=out_specs, check_vma=False)
```

```python
import functools
import jax
import jax.numpy as jnp
from jax import lax
from jax.experimental import pallas as pl
from jax.experimental.pallas import tpu as pltpu
from jax.sharding import PartitionSpec as P

HD = 128
BLOCK = 256
LANES = 128
F32 = jnp.float32
BF16 = jnp.bfloat16
NN = ((1,), (0,))
NT = ((1,), (1,))
TN = ((0,), (0,))


def split(x):
    high = x.astype(BF16)
    return high, (x - high.astype(F32)).astype(BF16)


def mul(left, right, dims):
    return lax.dot_general(left, right, (dims, ((), ())), preferred_element_type=F32)


def beside(*parts):
    return jnp.concatenate(parts, axis=1)


def product_nt(left, right):
    return mul(beside(*left), beside(right[0], right[0]), NT) + mul(left[0], right[1], NT)


def product_nn(left, right):
    size = right[0].shape[1]
    wide = mul(left[0], beside(*right), NN)
    return wide[:, :size] + wide[:, size:] + mul(left[1], right[0], NN)


def product_tn(left, right):
    rows, cols = left[0].shape[1], right[0].shape[1]
    wide = mul(beside(*left), beside(*right), TN)
    return wide[:rows, :cols] + wide[:rows, cols:] + wide[rows:, :cols]


def state_operand(state, transposed):
    high, low = split(state)
    if transposed:
        return jnp.concatenate([beside(high, high), beside(low, jnp.zeros_like(low))], axis=0)
    return jnp.concatenate([beside(high, low), beside(high, jnp.zeros_like(low))], axis=0)


def product_state(left, operand, transposed):
    wide = mul(beside(*left), operand, NT if transposed else NN)
    return wide[:, :HD] + wide[:, HD:]


def heads(width):
    return [slice(h * HD, (h + 1) * HD) for h in range(width // HD)]


def blocks(rows):
    size = min(BLOCK, rows)
    return [slice(n * size, (n + 1) * size) for n in range(rows // size)]


def call(body, name, outs, flops, operands, scratch=(), hbm_in=(), hbm_out=(), aliases=None):
    outs = [out if isinstance(out[0], tuple) else (out, F32) for out in outs]
    outs = [
        pltpu.HBM(*out) if i in hbm_out else jax.ShapeDtypeStruct(*out) for i, out in enumerate(outs)
    ]
    moved = 2 * sum(x.size * x.dtype.itemsize for x in operands)
    operands = [
        pltpu.with_memory_space_constraint(x, pltpu.HBM) if i in hbm_in else x for i, x in enumerate(operands)
    ]
    place = lambda far: pl.BlockSpec(memory_space=pltpu.HBM if far else pltpu.VMEM)
    return pl.pallas_call(
        body,
        out_shape=outs,
        in_specs=[place(i in hbm_in) for i in range(len(operands))],
        out_specs=[place(i in hbm_out) for i in range(len(outs))],
        scratch_shapes=list(scratch),
        input_output_aliases=aliases or {},
        name=name,
        cost_estimate=pl.CostEstimate(flops=flops, bytes_accessed=moved, transcendentals=0),
        compiler_params=pltpu.CompilerParams(vmem_limit_bytes=16 * 1024 * 1024),
    )(*operands)


def my_core():
    return lax.axis_index("seq") % 2


def half_cols(half, mine, start=0, size=None):
    which = my_core() if mine else 1 - my_core()
    return pl.ds(pl.multiple_of(which * half + start, LANES), size or half)


def causal_mask(size, transposed=False):
    row = lax.broadcasted_iota(jnp.int32, (size, size), 0)
    col = lax.broadcasted_iota(jnp.int32, (size, size), 1)
    return row <= col if transposed else row >= col


def block_states(k_ref, v_ref, mine, total_ref, before_ref, ready=None):
    rows, width = k_ref.shape
    half = width // 2
    count = len(blocks(rows))
    for n, row in enumerate(blocks(rows)):
        if ready:
            ready(n)
        for head in heads(half):
            col = half_cols(half, mine, head.start, HD)
            state = product_tn(split(k_ref[row, col]), split(v_ref[row, col]))
            if n > 0:
                state = state + before_ref[n - 1, head, :]
            if n + 1 < count:
                before_ref[n, head, :] = state
            else:
                total_ref[head, :] = state


def key_states_other(k_hbm, v_hbm, gain_hbm, total_ref, before_ref, k_ref, v_ref, gain_ref, sems, gain_sem):
    gain_copy = pltpu.make_async_copy(gain_hbm, gain_ref, gain_sem)
    copies = []
    for n, row in enumerate(blocks(k_ref.shape[0])):
        copies.append([
            pltpu.make_async_copy(far.at[row], near.at[row], sems.at[i, n])
            for i, (far, near) in enumerate(((k_hbm, k_ref), (v_hbm, v_ref)))
        ])
        for copy in copies[n]:
            copy.start()
    gain_copy.start()

    def ready(n):
        for copy in copies[n]:
            copy.wait()

    block_states(k_ref, v_ref, False, total_ref, before_ref, ready)
    gain_copy.wait()


def key_states_mine(k_ref, v_ref, q_ref, cot_ref, gain_ref, total_ref, before_ref, mine_ref, other_ref):
    half = k_ref.shape[1] // 2
    block_states(k_ref, v_ref, True, total_ref, before_ref)
    for mine, pack_ref in ((True, mine_ref), (False, other_ref)):
        col = half_cols(half, mine)
        pack_ref[:, :half] = q_ref[:, col]
        pack_ref[:, half:] = gain_ref[:, col] * cot_ref[:, col]


def attend_local(pack_mine_ref, pack_other_ref, k_ref, v_ref, before_mine_ref, before_other_ref, mine_ref, other_ref):
    rows, width = k_ref.shape
    half = width // 2
    parts = ((False, pack_other_ref, before_other_ref, other_ref), (True, pack_mine_ref, before_mine_ref, mine_ref))
    for mine, pack_ref, before_ref, out_ref in parts:
        for head in heads(half):
            col = half_cols(half, mine, head.start, HD)
            for n, row in enumerate(blocks(rows)):
                query = split(pack_ref[row, head])
                scores = product_nt(query, split(k_ref[row, col]))
                scores = jnp.where(causal_mask(scores.shape[0]), scores, 0.0)
                out = product_nn(split(scores), split(v_ref[row, col]))
                if n > 0:
                    out = out + product_state(query, state_operand(before_ref[n - 1, head, :], False), False)
                out_ref[row, head] = out


def attend_state(own_ref, own_local_ref, sib_ref, sib_local_ref, keep_ref, give_ref, own_out_ref, sib_out_ref, sums_ref):
    rows, width = own_ref.shape
    half = width // 2
    count = rows // LANES
    lane = lax.broadcasted_iota(jnp.int32, (LANES, LANES), 1)
    for core, pack_ref, local_ref, state_ref, out_ref in (
        (my_core(), own_ref, own_local_ref, keep_ref, own_out_ref),
        (1 - my_core(), sib_ref, sib_local_ref, give_ref, sib_out_ref),
    ):
        tile = jnp.zeros((LANES, LANES), F32)
        states = [state_operand(state_ref[head, :], False) for head in heads(half)]
        for n, row in enumerate(blocks(rows)):
            for head, state in zip(heads(half), states):
                out_ref[row, head] = local_ref[row, head] + product_state(split(pack_ref[row, head]), state, False)
        for j in range(count):
            row = slice(j * LANES, (j + 1) * LANES)
            out = out_ref[row, :]
            squares = jnp.sum(out * out, axis=1, keepdims=True)
            cross = jnp.sum(pack_ref[row, half:] * out, axis=1, keepdims=True)
            tile = jnp.where(lane == j, squares, tile)
            tile = jnp.where(lane == count + j, cross, tile)
        sums_ref[pl.ds(pl.multiple_of(core * 2 * count, 2 * count), 2 * count), :] = tile.T[: 2 * count]


def row_factors(full_width, rows, given_ref, got_ref, own):
    count = rows // LANES
    core = my_core() if own else 1 - my_core()
    place = pl.ds(pl.multiple_of(core * 2 * count, 2 * count), 2 * count)
    sums = given_ref[place, :] + got_ref[place, :]
    inverse = lax.rsqrt(sums[:count] / full_width + 1e-06)
    factor = inverse * inverse * inverse * (sums[count:] / full_width)
    both = jnp.concatenate([inverse, factor], axis=0)
    tile = jnp.concatenate([both] * (LANES // both.shape[0]), axis=0).T
    return [(tile[:, j : j + 1], tile[:, count + j : count + j + 1]) for j in range(count)]


def grad_of_block(factors, scaled, attended, row):
    parts = []
    for i in range((row.stop - row.start) // LANES):
        part = slice(i * LANES, (i + 1) * LANES)
        inverse, factor = factors[row.start // LANES + i]
        parts.append(inverse * scaled[part] - attended[part] * factor)
    return jnp.concatenate(parts, axis=0)


def grad_states(full_width, given_ref, got_ref, own_ref, sib_ref, own_att_ref, sib_att_ref, pair_ref, own_total_ref, sib_total_ref, after_ref, high_ref, low_ref):
    rows, width = own_ref.shape
    half = width // 2
    for own, pack_ref, att_ref, total_ref in ((False, sib_ref, sib_att_ref, sib_total_ref), (True, own_ref, own_att_ref, own_total_ref)):
        factors = row_factors(full_width, rows, given_ref, got_ref, own)
        for head in heads(half):
            total = None
            for n, row in reversed(list(enumerate(blocks(rows)))):
                scaled = pack_ref[row, half + head.start : half + head.stop]
                grad = split(grad_of_block(factors, scaled, att_ref[row, head], row))
                if own:
                    high_ref[row, head], low_ref[row, head] = grad
                state = product_tn(split(pack_ref[row, head]), grad)
                total = state if total is None else total + state
                if own and n > 0:
                    after_ref[n - 1, head, :] = total
            total_ref[head, :] = total
    pair_ref[...] = own_total_ref[...] + sib_total_ref[...]


def grads_local(full_width, given_ref, got_ref, high_ref, low_ref, local_ref, pack_mine_ref, pack_other_ref, k_ref, v_ref, keep_ref, before_mine_ref, before_other_ref, total_ref, gq_hbm, gk_ref, gv_ref, after_ref, same_total_ref, gq_ref, other_high, other_low, sems):
    rows, width = k_ref.shape
    half = width // 2
    sums_rows = 4 * rows // LANES
    same_total_ref[...] = total_ref[...]
    factors = row_factors(full_width, rows, given_ref, got_ref, True)
    copies = []
    for mine in (True, False):
        pack_ref, before_ref = (pack_mine_ref, before_mine_ref) if mine else (pack_other_ref, before_other_ref)
        for head in heads(half):
            col = half_cols(half, mine, head.start, HD)
            if mine:
                state = keep_ref[head, :]
            else:
                state = got_ref[sums_rows + head.start : sums_rows + head.stop, :]
                operand = state_operand(state, False)
                total = None
            for n, row in reversed(list(enumerate(blocks(rows)))):
                if mine:
                    grad = high_ref[row, head], low_ref[row, head]
                else:
                    query = split(pack_ref[row, head])
                    attended = local_ref[row, head] + product_state(query, operand, False)
                    scaled = pack_ref[row, half + head.start : half + head.stop]
                    grad = split(grad_of_block(factors, scaled, attended, row))
                    other_high[row, head], other_low[row, head] = grad
                    if n > 0:
                        more = product_tn(query, grad)
                        total = more if total is None else total + more
                        after_ref[n - 1, head, :] = total
                here = state_operand(state if n == 0 else state + before_ref[n - 1, head, :], True)
                mixing = product_nt(grad, split(v_ref[row, col]))
                mixing = jnp.where(causal_mask(row.stop - row.start), mixing, 0.0)
                gq_ref[row, col] = product_nn(split(mixing), split(k_ref[row, col])) + product_state(grad, here, True)
                copies.append(pltpu.make_async_copy(gq_ref.at[row, col], gq_hbm.at[row, col], sems.at[len(copies)]))
                copies[-1].start()
    for mine in (True, False):
        pack_ref = pack_mine_ref if mine else pack_other_ref
        for head in heads(half):
            col = half_cols(half, mine, head.start, HD)
            place = head if mine else slice(half + head.start, half + head.stop)
            for row in blocks(rows):
                grad = (high_ref[row, head], low_ref[row, head]) if mine else (other_high[row, head], other_low[row, head])
                query, key, value = split(pack_ref[row, head]), split(k_ref[row, col]), split(v_ref[row, col])
                mask = causal_mask(row.stop - row.start, True)
                mixing = jnp.where(mask, product_nt(value, grad), 0.0)
                gk_ref[row, place] = product_nn(split(mixing), query)
                scores = jnp.where(mask, product_nt(key, query), 0.0)
                gv_ref[row, place] = product_nn(split(scores), grad)
    for copy in copies:
        copy.wait()


def grads_state(mine, k_ref, v_ref, gk_local_ref, gv_local_ref, state_ref, after_ref, *refs):
    gk_hbm, gv_hbm, gk_ref, gv_ref, sems = refs[-5:]
    rows, width = k_ref.shape
    half = width // 2
    last = len(blocks(rows)) - 1
    copies = []

    def leave(near, far, row, head, col):
        copies.append(pltpu.make_async_copy(near.at[row, head], far.at[row, col], sems.at[len(copies)]))
        copies[-1].start()

    for head in heads(half):
        col = half_cols(half, mine, head.start, HD)
        place = head if mine else slice(half + head.start, half + head.stop)
        for n, row in enumerate(blocks(rows)):
            here = state_ref[head, :] if n == last else state_ref[head, :] + after_ref[n, head, :]
            gk_ref[row, head] = gk_local_ref[row, place] + product_state(split(v_ref[row, col]), state_operand(here, True), True)
            leave(gk_ref, gk_hbm, row, head, col)
            gv_ref[row, head] = gv_local_ref[row, place] + product_state(split(k_ref[row, col]), state_operand(here, False), False)
            leave(gv_ref, gv_hbm, row, head, col)
    for copy in copies:
        copy.wait()


def swap(x, axis, distance):
    count = lax.axis_size(axis)
    return lax.ppermute(x, axis, [(i, i ^ distance) for i in range(count)])


def from_other_chips(pair, reverse):
    chip = lax.axis_index("seq") // 2
    chips = lax.axis_size("seq") // 2
    total = jnp.zeros_like(pair)
    ahead = lambda d: (chip ^ d) > chip if reverse else (chip ^ d) < chip
    if chips <= 4:
        got = [(d, swap(pair, "seq", 2 * d)) for d in reversed(range(1, chips))]
        for d, part in got:
            total = total + jnp.where(ahead(d), part, 0.0)
        return total
    d = 1
    while d < chips:
        part = swap(pair, "seq", 2 * d)
        total = total + jnp.where(ahead(d), part, 0.0)
        pair = pair + part
        d *= 2
    return total


def sum_over_heads(x):
    count = lax.axis_size("head")
    if count > 4 or count & (count - 1):
        return lax.psum(x, "head")
    parts = [swap(x, "head", d) for d in reversed(range(1, count))]
    for part in parts:
        x = x + part
    return x


def shards(queries, keys, values, cotangent, gain):
    rows, width = queries.shape
    full_width = width * lax.axis_size("head")
    half = width // 2
    count = len(blocks(rows))
    units = count * (width // HD)
    square = rows * width * HD * 2 * 3
    whole, halves, state = (rows, width), (rows, half), (half, HD)
    inner = (max(count - 1, 1), half, HD)
    first = lax.axis_index("seq") % 2 == 0
    gain = gain.reshape(1, width)

    other, before_other, near_keys, near_values, gain = call(
        key_states_other, "key_states_other", [state, inner, whole, whole, (1, width)], square // 2,
        [keys, values, gain], [pltpu.SemaphoreType.DMA((2, count)), pltpu.SemaphoreType.DMA], hbm_in=(0, 1, 2),
    )
    from_pair = swap(other, "seq", 1)
    mine, before_mine, pack_mine, pack_other = call(
        key_states_mine, "key_states_mine", [state, inner, whole, whole], square // 2,
        [near_keys, near_values, queries, cotangent, gain],
    )
    sibling = swap(pack_other, "seq", 1)
    earlier = from_other_chips(mine + from_pair, False)
    keep = earlier + jnp.where(first, 0.0, from_pair)
    give = earlier + jnp.where(first, mine, 0.0)
    local_mine, local_other = call(
        attend_local, "attend_local", [halves, halves], 5 * square,
        [pack_mine, pack_other, near_keys, near_values, before_mine, before_other],
    )
    sibling_local = swap(local_other, "seq", 1)
    attended, sibling_attended, sums = call(
        attend_state, "attend_state", [halves, halves, (4 * rows // LANES, LANES)], square,
        [pack_mine, local_mine, sibling, sibling_local, keep, give],
    )
    given = jnp.concatenate([sum_over_heads(sums), give], axis=0)
    got = swap(given, "seq", 1)
    pair, own_grad, sibling_grad, after_mine, high, low = call(
        functools.partial(grad_states, full_width), "grad_states",
        [state, state, state, inner, (halves, BF16), (halves, BF16)], square,
        [given, got, pack_mine, sibling, attended, sibling_attended],
    )
    later = from_other_chips(pair, True)
    grad_q, local_k, local_v, after_other, own_grad = call(
        functools.partial(grads_local, full_width), "grads_local", [whole, whole, whole, inner, state], 14 * square,
        [given, got, high, low, local_other, pack_mine, pack_other, keys, values, keep, before_mine, before_other, own_grad],
        [pltpu.VMEM(whole, F32), pltpu.VMEM(halves, BF16), pltpu.VMEM(halves, BF16), pltpu.SemaphoreType.DMA((units,))],
        hbm_out=(0,),
    )
    keep_later = later + jnp.where(first, sibling_grad, 0.0)
    got_later = swap(later + jnp.where(first, 0.0, own_grad), "seq", 1)
    scratch = [pltpu.VMEM(halves, F32), pltpu.VMEM(halves, F32), pltpu.SemaphoreType.DMA((units,))]
    grad_k, grad_v = call(
        functools.partial(grads_state, True), "grads_state_mine", [whole] * 2, square,
        [keys, values, local_k, local_v, keep_later, after_mine], scratch, hbm_out=(0, 1),
    )
    grad_k, grad_v = call(
        functools.partial(grads_state, False), "grads_state_other", [whole] * 2, square,
        [keys, values, local_k, local_v, got_later, after_other, grad_k, grad_v], scratch,
        hbm_in=(6, 7), hbm_out=(0, 1), aliases={6: 0, 7: 1},
    )
    return grad_q, grad_k, grad_v


def solution(mesh):
    in_specs = (P("seq", "head"), P("seq", "head"), P("seq", "head"), P("seq", "head"), P("head"))
    out_specs = (P("seq", "head"), P("seq", "head"), P("seq", "head"))
    return jax.shard_map(shards, mesh=mesh, in_specs=in_specs, out_specs=out_specs, check_vma=False)
```

```python
import functools
import jax
import jax.numpy as jnp
from jax import lax
from jax.experimental import pallas as pl
from jax.experimental.pallas import tpu as pltpu
from jax.sharding import PartitionSpec as P

HD = 128
BLOCK = 256
LANES = 128
F32 = jnp.float32
BF16 = jnp.bfloat16
NN = ((1,), (0,))
NT = ((1,), (1,))
TN = ((0,), (0,))


def split(x):
    high = x.astype(BF16)
    return high, (x - high.astype(F32)).astype(BF16)


def mul(left, right, dims):
    return lax.dot_general(left, right, (dims, ((), ())), preferred_element_type=F32)


def beside(*parts):
    return jnp.concatenate(parts, axis=1)


def product_nt(left, right):
    return mul(beside(*left), beside(right[0], right[0]), NT) + mul(left[0], right[1], NT)


def product_nn(left, right):
    size = right[0].shape[1]
    wide = mul(left[0], beside(*right), NN)
    return wide[:, :size] + wide[:, size:] + mul(left[1], right[0], NN)


def product_tn(left, right):
    rows, cols = left[0].shape[1], right[0].shape[1]
    wide = mul(beside(*left), beside(*right), TN)
    return wide[:rows, :cols] + wide[:rows, cols:] + wide[rows:, :cols]


def state_operand(state, transposed):
    high, low = split(state)
    if transposed:
        return jnp.concatenate([beside(high, high), beside(low, jnp.zeros_like(low))], axis=0)
    return jnp.concatenate([beside(high, low), beside(high, jnp.zeros_like(low))], axis=0)


def product_state(left, operand, transposed):
    wide = mul(beside(*left), operand, NT if transposed else NN)
    return wide[:, :HD] + wide[:, HD:]


def heads(width):
    return [slice(h * HD, (h + 1) * HD) for h in range(width // HD)]


def blocks(rows):
    size = min(BLOCK, rows)
    return [slice(n * size, (n + 1) * size) for n in range(rows // size)]


def call(body, name, outs, flops, operands, scratch=(), hbm_in=(), hbm_out=(), aliases=None):
    outs = [out if isinstance(out[0], tuple) else (out, F32) for out in outs]
    outs = [
        pltpu.HBM(*out) if i in hbm_out else jax.ShapeDtypeStruct(*out) for i, out in enumerate(outs)
    ]
    moved = 2 * sum(x.size * x.dtype.itemsize for x in operands)
    operands = [
        pltpu.with_memory_space_constraint(x, pltpu.HBM) if i in hbm_in else x for i, x in enumerate(operands)
    ]
    place = lambda far: pl.BlockSpec(memory_space=pltpu.HBM if far else pltpu.VMEM)
    return pl.pallas_call(
        body,
        out_shape=outs,
        in_specs=[place(i in hbm_in) for i in range(len(operands))],
        out_specs=[place(i in hbm_out) for i in range(len(outs))],
        scratch_shapes=list(scratch),
        input_output_aliases=aliases or {},
        name=name,
        cost_estimate=pl.CostEstimate(flops=flops, bytes_accessed=moved, transcendentals=0),
        compiler_params=pltpu.CompilerParams(vmem_limit_bytes=16 * 1024 * 1024),
    )(*operands)


def my_core():
    return lax.axis_index("seq") % 2


def on_grid():
    return lax.axis_size("seq") == 8


def my_half():
    place = lax.axis_index("seq")
    return (place + place // 2) % 2 if on_grid() else place % 2


def half_cols(half, mine, start=0, size=None):
    which = my_half() if mine else 1 - my_half()
    return pl.ds(pl.multiple_of(which * half + start, LANES), size or half)


def causal_mask(size, transposed=False):
    row = lax.broadcasted_iota(jnp.int32, (size, size), 0)
    col = lax.broadcasted_iota(jnp.int32, (size, size), 1)
    return row <= col if transposed else row >= col


def block_states(k_ref, v_ref, mine, total_ref, before_ref, ready=None):
    rows, width = k_ref.shape
    half = width // 2
    count = len(blocks(rows))
    for n, row in enumerate(blocks(rows)):
        if ready:
            ready(n)
        for head in heads(half):
            col = half_cols(half, mine, head.start, HD)
            state = product_tn(split(k_ref[row, col]), split(v_ref[row, col]))
            if n > 0:
                state = state + before_ref[n - 1, head, :]
            if n + 1 < count:
                before_ref[n, head, :] = state
            else:
                total_ref[head, :] = state


def key_states_other(k_hbm, v_hbm, gain_hbm, total_ref, before_ref, k_ref, v_ref, gain_ref, sems, gain_sem):
    gain_copy = pltpu.make_async_copy(gain_hbm, gain_ref, gain_sem)
    copies = []
    for n, row in enumerate(blocks(k_ref.shape[0])):
        copies.append([
            pltpu.make_async_copy(far.at[row], near.at[row], sems.at[i, n])
            for i, (far, near) in enumerate(((k_hbm, k_ref), (v_hbm, v_ref)))
        ])
        for copy in copies[n]:
            copy.start()
    gain_copy.start()

    def ready(n):
        for copy in copies[n]:
            copy.wait()

    block_states(k_ref, v_ref, False, total_ref, before_ref, ready)
    gain_copy.wait()


def key_states_mine(k_ref, v_ref, q_ref, cot_ref, gain_ref, total_ref, before_ref, mine_ref, other_ref):
    half = k_ref.shape[1] // 2
    block_states(k_ref, v_ref, True, total_ref, before_ref)
    for mine, pack_ref in ((True, mine_ref), (False, other_ref)):
        col = half_cols(half, mine)
        pack_ref[:, :half] = q_ref[:, col]
        pack_ref[:, half:] = gain_ref[:, col] * cot_ref[:, col]


def attend_local(pack_mine_ref, pack_other_ref, k_ref, v_ref, before_mine_ref, before_other_ref, mine_ref, other_ref):
    rows, width = k_ref.shape
    half = width // 2
    parts = ((False, pack_other_ref, before_other_ref, other_ref), (True, pack_mine_ref, before_mine_ref, mine_ref))
    for mine, pack_ref, before_ref, out_ref in parts:
        for head in heads(half):
            col = half_cols(half, mine, head.start, HD)
            for n, row in enumerate(blocks(rows)):
                query = split(pack_ref[row, head])
                scores = product_nt(query, split(k_ref[row, col]))
                scores = jnp.where(causal_mask(scores.shape[0]), scores, 0.0)
                out = product_nn(split(scores), split(v_ref[row, col]))
                if n > 0:
                    out = out + product_state(query, state_operand(before_ref[n - 1, head, :], False), False)
                out_ref[row, head] = out


def attend_state(own_ref, own_local_ref, sib_ref, sib_local_ref, keep_ref, give_ref, own_out_ref, sib_out_ref, sums_ref):
    rows, width = own_ref.shape
    half = width // 2
    count = rows // LANES
    lane = lax.broadcasted_iota(jnp.int32, (LANES, LANES), 1)
    for core, pack_ref, local_ref, state_ref, out_ref in (
        (my_core(), own_ref, own_local_ref, keep_ref, own_out_ref),
        (1 - my_core(), sib_ref, sib_local_ref, give_ref, sib_out_ref),
    ):
        tile = jnp.zeros((LANES, LANES), F32)
        states = [state_operand(state_ref[head, :], False) for head in heads(half)]
        for n, row in enumerate(blocks(rows)):
            for head, state in zip(heads(half), states):
                out_ref[row, head] = local_ref[row, head] + product_state(split(pack_ref[row, head]), state, False)
        for j in range(count):
            row = slice(j * LANES, (j + 1) * LANES)
            out = out_ref[row, :]
            squares = jnp.sum(out * out, axis=1, keepdims=True)
            cross = jnp.sum(pack_ref[row, half:] * out, axis=1, keepdims=True)
            tile = jnp.where(lane == j, squares, tile)
            tile = jnp.where(lane == count + j, cross, tile)
        sums_ref[pl.ds(pl.multiple_of(core * 2 * count, 2 * count), 2 * count), :] = tile.T[: 2 * count]


def attend_other(pair_sums_ref, got_ref, pack_ref, local_ref, out_ref, same_sums_ref):
    same_sums_ref[...] = pair_sums_ref[...]
    start = pair_sums_ref.shape[0]
    rows, half = local_ref.shape
    for head in heads(half):
        operand = state_operand(got_ref[start + head.start : start + head.stop, :], False)
        for row in blocks(rows):
            out_ref[row, head] = local_ref[row, head] + product_state(split(pack_ref[row, head]), operand, False)


def row_factors(full_width, rows, sums_ref, own):
    count = rows // LANES
    core = my_core() if own else 1 - my_core()
    sums = sums_ref[pl.ds(pl.multiple_of(core * 2 * count, 2 * count), 2 * count), :]
    inverse = lax.rsqrt(sums[:count] / full_width + 1e-06)
    factor = inverse * inverse * inverse * (sums[count:] / full_width)
    both = jnp.concatenate([inverse, factor], axis=0)
    tile = jnp.concatenate([both] * (LANES // both.shape[0]), axis=0).T
    return [(tile[:, j : j + 1], tile[:, count + j : count + j + 1]) for j in range(count)]


def grad_of_block(factors, scaled, attended, row):
    parts = []
    for i in range((row.stop - row.start) // LANES):
        part = slice(i * LANES, (i + 1) * LANES)
        inverse, factor = factors[row.start // LANES + i]
        parts.append(inverse * scaled[part] - attended[part] * factor)
    return jnp.concatenate(parts, axis=0)


def grad_states(full_width, sums_ref, own_ref, sib_ref, own_att_ref, sib_att_ref, pair_ref, own_total_ref, sib_total_ref, after_ref, high_ref, low_ref):
    rows, width = own_ref.shape
    half = width // 2
    for own, pack_ref, att_ref, total_ref in ((False, sib_ref, sib_att_ref, sib_total_ref), (True, own_ref, own_att_ref, own_total_ref)):
        factors = row_factors(full_width, rows, sums_ref, own)
        for head in heads(half):
            total = None
            for n, row in reversed(list(enumerate(blocks(rows)))):
                scaled = pack_ref[row, half + head.start : half + head.stop]
                grad = split(grad_of_block(factors, scaled, att_ref[row, head], row))
                if own:
                    high_ref[row, head], low_ref[row, head] = grad
                state = product_tn(split(pack_ref[row, head]), grad)
                total = state if total is None else total + state
                if own and n > 0:
                    after_ref[n - 1, head, :] = total
            total_ref[head, :] = total
    pair_ref[...] = own_total_ref[...] + sib_total_ref[...]


def grads_local(full_width, sums_ref, got_ref, high_ref, low_ref, att_other_ref, pack_mine_ref, pack_other_ref, k_ref, v_ref, keep_ref, before_mine_ref, before_other_ref, total_ref, gq_hbm, gk_ref, gv_ref, after_ref, same_total_ref, gq_ref, other_high, other_low, sems):
    rows, width = k_ref.shape
    half = width // 2
    sums_rows = 4 * rows // LANES
    same_total_ref[...] = total_ref[...]
    factors = row_factors(full_width, rows, sums_ref, True)
    copies = []
    for mine in (True, False):
        pack_ref, before_ref = (pack_mine_ref, before_mine_ref) if mine else (pack_other_ref, before_other_ref)
        for head in heads(half):
            col = half_cols(half, mine, head.start, HD)
            if mine:
                state = keep_ref[head, :]
            else:
                state = got_ref[sums_rows + head.start : sums_rows + head.stop, :]
                total = None
            for n, row in reversed(list(enumerate(blocks(rows)))):
                if mine:
                    grad = high_ref[row, head], low_ref[row, head]
                else:
                    scaled = pack_ref[row, half + head.start : half + head.stop]
                    grad = split(grad_of_block(factors, scaled, att_other_ref[row, head], row))
                    other_high[row, head], other_low[row, head] = grad
                    if n > 0:
                        more = product_tn(split(pack_ref[row, head]), grad)
                        total = more if total is None else total + more
                        after_ref[n - 1, head, :] = total
                here = state_operand(state if n == 0 else state + before_ref[n - 1, head, :], True)
                mixing = product_nt(grad, split(v_ref[row, col]))
                mixing = jnp.where(causal_mask(row.stop - row.start), mixing, 0.0)
                gq_ref[row, col] = product_state(grad, here, True)
                gq_ref[row, col] += product_nn(split(mixing), split(k_ref[row, col]))
                copies.append(pltpu.make_async_copy(gq_ref.at[row, col], gq_hbm.at[row, col], sems.at[len(copies)]))
                copies[-1].start()
    for mine in (True, False):
        pack_ref = pack_mine_ref if mine else pack_other_ref
        for head in heads(half):
            col = half_cols(half, mine, head.start, HD)
            place = head if mine else slice(half + head.start, half + head.stop)
            for row in blocks(rows):
                grad = (high_ref[row, head], low_ref[row, head]) if mine else (other_high[row, head], other_low[row, head])
                query, key, value = split(pack_ref[row, head]), split(k_ref[row, col]), split(v_ref[row, col])
                mask = causal_mask(row.stop - row.start, True)
                mixing = jnp.where(mask, product_nt(value, grad), 0.0)
                gk_ref[row, place] = product_nn(split(mixing), query)
                scores = jnp.where(mask, product_nt(key, query), 0.0)
                gv_ref[row, place] = product_nn(split(scores), grad)
    for copy in copies:
        copy.wait()


def grads_state(mine, k_ref, v_ref, gk_local_ref, gv_local_ref, state_ref, after_ref, *refs):
    gk_hbm, gv_hbm, gk_ref, gv_ref, sems = refs[-5:]
    rows, width = k_ref.shape
    half = width // 2
    last = len(blocks(rows)) - 1
    copies = []

    def leave(near, far, row, head, col):
        copies.append(pltpu.make_async_copy(near.at[row, head], far.at[row, col], sems.at[len(copies)]))
        copies[-1].start()

    for head in heads(half):
        col = half_cols(half, mine, head.start, HD)
        place = head if mine else slice(half + head.start, half + head.stop)
        for n, row in enumerate(blocks(rows)):
            here = state_ref[head, :] if n == last else state_ref[head, :] + after_ref[n, head, :]
            gk_ref[row, head] = gk_local_ref[row, place] + product_state(split(v_ref[row, col]), state_operand(here, True), True)
            leave(gk_ref, gk_hbm, row, head, col)
            gv_ref[row, head] = gv_local_ref[row, place] + product_state(split(k_ref[row, col]), state_operand(here, False), False)
            leave(gv_ref, gv_hbm, row, head, col)
    for copy in copies:
        copy.wait()


def swap(x, axis, distance):
    count = lax.axis_size(axis)
    return lax.ppermute(x, axis, [(i, i ^ distance) for i in range(count)])


def from_other_chips(pair, reverse):
    place = lax.axis_index("seq")
    chip = place // 2
    ahead = lambda d: (chip ^ d) > chip if reverse else (chip ^ d) < chip
    total = jnp.zeros_like(pair)
    if on_grid():
        got = [(d, swap(pair, "seq", 2 * d + d % 2)) for d in (3, 2, 1)]
        for d, part in got:
            total = total + jnp.where(ahead(d), part, 0.0)
        return total
    d = 1
    while d < lax.axis_size("seq") // 2:
        part = swap(pair, "seq", 2 * d)
        total = total + jnp.where(ahead(d), part, 0.0)
        pair = pair + part
        d *= 2
    return total


def sum_over_heads(x, same_x):
    count = lax.axis_size("head")
    if count > 4 or count & (count - 1):
        return lax.psum(same_x, "head")
    parts = []
    seqs = range(lax.axis_size("seq"))
    for d in reversed(range(1, count)):
        pairs = [(i * count + z, (i ^ 1) * count + (z ^ d)) for i in seqs for z in range(count)]
        parts.append(lax.ppermute(x, ("seq", "head"), pairs))
    for part in parts:
        same_x = same_x + part
    return same_x


def shards(queries, keys, values, cotangent, gain):
    rows, width = queries.shape
    full_width = width * lax.axis_size("head")
    half = width // 2
    count = len(blocks(rows))
    units = count * (width // HD)
    square = rows * width * HD * 2 * 3
    whole, halves, state = (rows, width), (rows, half), (half, HD)
    inner = (max(count - 1, 1), half, HD)
    first = lax.axis_index("seq") % 2 == 0
    gain = gain.reshape(1, width)

    other, before_other, near_keys, near_values, gain = call(
        key_states_other, "key_states_other", [state, inner, whole, whole, (1, width)], square // 2,
        [keys, values, gain], [pltpu.SemaphoreType.DMA((2, count)), pltpu.SemaphoreType.DMA], hbm_in=(0, 1, 2),
    )
    from_pair = swap(other, "seq", 1)
    mine, before_mine, pack_mine, pack_other = call(
        key_states_mine, "key_states_mine", [state, inner, whole, whole], square // 2,
        [near_keys, near_values, queries, cotangent, gain],
    )
    sibling = swap(pack_other, "seq", 1)
    earlier = from_other_chips(mine + from_pair, False)
    keep = earlier + jnp.where(first, 0.0, from_pair)
    give = earlier + jnp.where(first, mine, 0.0)
    local_mine, local_other = call(
        attend_local, "attend_local", [halves, halves], 5 * square,
        [pack_mine, pack_other, near_keys, near_values, before_mine, before_other],
    )
    sibling_local = swap(local_other, "seq", 1)
    attended, sibling_attended, sums = call(
        attend_state, "attend_state", [halves, halves, (4 * rows // LANES, LANES)], square,
        [pack_mine, local_mine, sibling, sibling_local, keep, give],
    )
    given = jnp.concatenate([sums, give], axis=0)
    got = swap(given, "seq", 1)
    pair_sums = given[: sums.shape[0]] + got[: sums.shape[0]]
    attended_other, same_pair_sums = call(
        attend_other, "attend_other", [halves, sums.shape], square // 2, [pair_sums, got, pack_other, local_other]
    )
    sums = sum_over_heads(pair_sums, same_pair_sums)
    pair, own_grad, sibling_grad, after_mine, high, low = call(
        functools.partial(grad_states, full_width), "grad_states",
        [state, state, state, inner, (halves, BF16), (halves, BF16)], square,
        [sums, pack_mine, sibling, attended, sibling_attended],
    )
    later = from_other_chips(pair, True)
    grad_q, local_k, local_v, after_other, own_grad = call(
        functools.partial(grads_local, full_width), "grads_local", [whole, whole, whole, inner, state], 14 * square,
        [sums, got, high, low, attended_other, pack_mine, pack_other, keys, values, keep, before_mine, before_other, own_grad],
        [pltpu.VMEM(whole, F32), pltpu.VMEM(halves, BF16), pltpu.VMEM(halves, BF16), pltpu.SemaphoreType.DMA((units,))],
        hbm_out=(0,),
    )
    keep_later = later + jnp.where(first, sibling_grad, 0.0)
    got_later = swap(later + jnp.where(first, 0.0, own_grad), "seq", 1)
    scratch = [pltpu.VMEM(halves, F32), pltpu.VMEM(halves, F32), pltpu.SemaphoreType.DMA((units,))]
    grad_k, grad_v = call(
        functools.partial(grads_state, True), "grads_state_mine", [whole] * 2, square,
        [keys, values, local_k, local_v, keep_later, after_mine], scratch, hbm_out=(0, 1),
    )
    grad_k, grad_v = call(
        functools.partial(grads_state, False), "grads_state_other", [whole] * 2, square,
        [keys, values, local_k, local_v, got_later, after_other, grad_k, grad_v], scratch,
        hbm_in=(6, 7), hbm_out=(0, 1), aliases={6: 0, 7: 1},
    )
    return grad_q, grad_k, grad_v


def solution(mesh):
    in_specs = (P("seq", "head"), P("seq", "head"), P("seq", "head"), P("seq", "head"), P("head"))
    out_specs = (P("seq", "head"), P("seq", "head"), P("seq", "head"))
    return jax.shard_map(shards, mesh=mesh, in_specs=in_specs, out_specs=out_specs, check_vma=False)
```

```python
import functools
import jax
import jax.numpy as jnp
from jax import lax
from jax.experimental import pallas as pl
from jax.experimental.pallas import tpu as pltpu
from jax.sharding import PartitionSpec as P

HD = 128
BLOCK = 256
LANES = 128
F32 = jnp.float32
BF16 = jnp.bfloat16
NN = ((1,), (0,))
NT = ((1,), (1,))
TN = ((0,), (0,))


def split(x):
    high = x.astype(BF16)
    return high, (x - high.astype(F32)).astype(BF16)


def mul(left, right, dims):
    return lax.dot_general(left, right, (dims, ((), ())), preferred_element_type=F32)


def beside(*parts):
    return jnp.concatenate(parts, axis=1)


def product_nt(left, right):
    return mul(beside(*left), beside(right[0], right[0]), NT) + mul(left[0], right[1], NT)


def product_nn(left, right):
    size = right[0].shape[1]
    wide = mul(left[0], beside(*right), NN)
    return wide[:, :size] + wide[:, size:] + mul(left[1], right[0], NN)


def product_tn(left, right):
    rows, cols = left[0].shape[1], right[0].shape[1]
    wide = mul(beside(*left), beside(*right), TN)
    return wide[:rows, :cols] + wide[:rows, cols:] + wide[rows:, :cols]


def state_operand(state, transposed):
    high, low = split(state)
    if transposed:
        return jnp.concatenate([beside(high, high), beside(low, jnp.zeros_like(low))], axis=0)
    return jnp.concatenate([beside(high, low), beside(high, jnp.zeros_like(low))], axis=0)


def product_state(left, operand, transposed):
    wide = mul(beside(*left), operand, NT if transposed else NN)
    return wide[:, :HD] + wide[:, HD:]


def heads(width):
    return [slice(h * HD, (h + 1) * HD) for h in range(width // HD)]


def blocks(rows):
    size = min(BLOCK, rows)
    return [slice(n * size, (n + 1) * size) for n in range(rows // size)]


def call(body, name, outs, flops, operands, scratch=(), hbm_in=(), hbm_out=(), aliases=None):
    outs = [out if isinstance(out[0], tuple) else (out, F32) for out in outs]
    outs = [
        pltpu.HBM(*out) if i in hbm_out else jax.ShapeDtypeStruct(*out) for i, out in enumerate(outs)
    ]
    moved = 2 * sum(x.size * x.dtype.itemsize for x in operands)
    operands = [
        pltpu.with_memory_space_constraint(x, pltpu.HBM) if i in hbm_in else x for i, x in enumerate(operands)
    ]
    place = lambda far: pl.BlockSpec(memory_space=pltpu.HBM if far else pltpu.VMEM)
    return pl.pallas_call(
        body,
        out_shape=outs,
        in_specs=[place(i in hbm_in) for i in range(len(operands))],
        out_specs=[place(i in hbm_out) for i in range(len(outs))],
        scratch_shapes=list(scratch),
        input_output_aliases=aliases or {},
        name=name,
        cost_estimate=pl.CostEstimate(flops=flops, bytes_accessed=moved, transcendentals=0),
        compiler_params=pltpu.CompilerParams(vmem_limit_bytes=16 * 1024 * 1024),
    )(*operands)


def my_core():
    return lax.axis_index("seq") % 2


def on_grid():
    return lax.axis_size("seq") == 8


def my_half():
    place = lax.axis_index("seq")
    return (place + place // 2) % 2 if on_grid() else place % 2


def half_cols(half, mine, start=0, size=None):
    which = my_half() if mine else 1 - my_half()
    return pl.ds(pl.multiple_of(which * half + start, LANES), size or half)


def causal_mask(size, transposed=False):
    row = lax.broadcasted_iota(jnp.int32, (size, size), 0)
    col = lax.broadcasted_iota(jnp.int32, (size, size), 1)
    return row <= col if transposed else row >= col


def block_states(k_ref, v_ref, mine, total_ref, before_ref, ready=None):
    rows, width = k_ref.shape
    half = width // 2
    count = len(blocks(rows))
    for n, row in enumerate(blocks(rows)):
        if ready:
            ready(n)
        for head in heads(half):
            col = half_cols(half, mine, head.start, HD)
            state = product_tn(split(k_ref[row, col]), split(v_ref[row, col]))
            if n > 0:
                state = state + before_ref[n - 1, head, :]
            if n + 1 < count:
                before_ref[n, head, :] = state
            else:
                total_ref[head, :] = state


def key_states_other(k_hbm, v_hbm, gain_hbm, total_ref, before_ref, k_ref, v_ref, gain_ref, sems, gain_sem):
    gain_copy = pltpu.make_async_copy(gain_hbm, gain_ref, gain_sem)
    copies = []
    for n, row in enumerate(blocks(k_ref.shape[0])):
        copies.append([
            pltpu.make_async_copy(far.at[row], near.at[row], sems.at[i, n])
            for i, (far, near) in enumerate(((k_hbm, k_ref), (v_hbm, v_ref)))
        ])
        for copy in copies[n]:
            copy.start()
    gain_copy.start()

    def ready(n):
        for copy in copies[n]:
            copy.wait()

    block_states(k_ref, v_ref, False, total_ref, before_ref, ready)
    gain_copy.wait()


def key_states_mine(k_ref, v_ref, q_ref, cot_ref, gain_ref, total_ref, before_ref, mine_ref, other_ref):
    half = k_ref.shape[1] // 2
    block_states(k_ref, v_ref, True, total_ref, before_ref)
    for mine, pack_ref in ((True, mine_ref), (False, other_ref)):
        col = half_cols(half, mine)
        pack_ref[:half, :] = q_ref[:, col].T
        pack_ref[half:, :] = (gain_ref[:, col] * cot_ref[:, col]).T


def state_times(state, query):
    left = split(state.T)
    twice = jnp.concatenate([query[0], query[0]], axis=0)
    return mul(beside(*left), twice, NN) + mul(left[0], query[1], NN)


def over_steps(left, right):
    rows, cols = left[0].shape[0], right[0].shape[0]
    wide = mul(jnp.concatenate(left, axis=0), jnp.concatenate(right, axis=0), NT)
    return wide[:rows, :cols] + wide[:rows, cols:] + wide[rows:, :cols]


def attend_local(pack_mine_ref, pack_other_ref, k_ref, v_ref, before_mine_ref, before_other_ref, mine_ref, other_ref):
    rows, width = k_ref.shape
    half = width // 2
    parts = ((False, pack_other_ref, before_other_ref, other_ref), (True, pack_mine_ref, before_mine_ref, mine_ref))
    for mine, pack_ref, before_ref, out_ref in parts:
        for head in heads(half):
            col = half_cols(half, mine, head.start, HD)
            for n, row in enumerate(blocks(rows)):
                query = split(pack_ref[head, row])
                key = split(k_ref[row, col])
                twice = jnp.concatenate([query[0], query[0]], axis=0)
                scores = mul(beside(*key), twice, NN) + mul(key[0], query[1], NN)
                scores = split(jnp.where(causal_mask(scores.shape[0], True), scores, 0.0))
                value = split(v_ref[row, col].T)
                out = mul(value[0], scores[0], NN) + mul(value[0], scores[1], NN) + mul(value[1], scores[0], NN)
                if n > 0:
                    out = out + state_times(before_ref[n - 1, head, :], query)
                out_ref[head, row] = out


def lane_rows(x):
    return [x[:, start : start + LANES] for start in range(0, x.shape[1], LANES)]


def attend_state(own_ref, own_local_ref, sib_ref, sib_local_ref, keep_ref, give_ref, own_out_ref, sib_out_ref, sums_ref):
    half, rows = own_local_ref.shape
    count = rows // LANES
    for core, pack_ref, local_ref, state_ref, out_ref in (
        (my_core(), own_ref, own_local_ref, keep_ref, own_out_ref),
        (1 - my_core(), sib_ref, sib_local_ref, give_ref, sib_out_ref),
    ):
        squares, cross = jnp.zeros((1, rows), F32), jnp.zeros((1, rows), F32)
        for head in heads(half):
            out = local_ref[head, :] + state_times(state_ref[head, :], split(pack_ref[head, :]))
            out_ref[head, :] = out
            scaled = pack_ref[half + head.start : half + head.stop, :]
            squares = squares + jnp.sum(out * out, axis=0, keepdims=True)
            cross = cross + jnp.sum(scaled * out, axis=0, keepdims=True)
        place = pl.ds(pl.multiple_of(core * 2 * count, 2 * count), 2 * count)
        sums_ref[place, :] = jnp.concatenate(lane_rows(squares) + lane_rows(cross), axis=0)


def attend_other(pair_sums_ref, got_ref, pack_ref, local_ref, out_ref, same_sums_ref):
    same_sums_ref[...] = pair_sums_ref[...]
    start = pair_sums_ref.shape[0]
    for head in heads(local_ref.shape[0]):
        state = got_ref[start + head.start : start + head.stop, :]
        out_ref[head, :] = local_ref[head, :] + state_times(state, split(pack_ref[head, :]))


def step_factors(full_width, rows, sums_ref, own):
    count = rows // LANES
    core = my_core() if own else 1 - my_core()
    sums = sums_ref[pl.ds(pl.multiple_of(core * 2 * count, 2 * count), 2 * count), :]
    inverse = lax.rsqrt(sums[:count] / full_width + 1e-06)
    factor = inverse * inverse * inverse * (sums[count:] / full_width)
    return [beside(*[x[j : j + 1, :] for j in range(count)]) for x in (inverse, factor)]


def gradient(factors, pack_ref, att_ref, head):
    half = att_ref.shape[0]
    scaled = pack_ref[half + head.start : half + head.stop, :]
    return split(factors[0] * scaled - factors[1] * att_ref[head, :])


def steps(parts, row):
    return [part[:, row] for part in parts]


def grad_states(full_width, sums_ref, own_ref, sib_ref, own_att_ref, sib_att_ref, pair_ref, own_total_ref, sib_total_ref, after_ref, high_ref, low_ref):
    half, rows = own_att_ref.shape
    for own, pack_ref, att_ref, total_ref in ((False, sib_ref, sib_att_ref, sib_total_ref), (True, own_ref, own_att_ref, own_total_ref)):
        factors = step_factors(full_width, rows, sums_ref, own)
        for head in heads(half):
            grad = gradient(factors, pack_ref, att_ref, head)
            query = split(pack_ref[head, :])
            total = None
            for n, row in reversed(list(enumerate(blocks(rows)))):
                state = over_steps(steps(grad, row), steps(query, row))
                total = state if total is None else total + state
                if own and n > 0:
                    after_ref[n - 1, head, :] = total
            if own:
                high_ref[head, :], low_ref[head, :] = grad
            total_ref[head, :] = total
    pair_ref[...] = own_total_ref[...] + sib_total_ref[...]


def grads_local(full_width, sums_ref, got_ref, high_ref, low_ref, att_other_ref, pack_mine_ref, pack_other_ref, k_ref, v_ref, keep_ref, before_mine_ref, before_other_ref, total_ref, gq_hbm, gk_ref, gv_ref, after_ref, same_total_ref, gq_ref, grad_high, grad_low, sems):
    rows, width = k_ref.shape
    half = width // 2
    sums_rows = 4 * rows // LANES
    same_total_ref[...] = total_ref[...]
    factors = step_factors(full_width, rows, sums_ref, True)
    copies = []
    for mine in (True, False):
        pack_ref, before_ref = (pack_mine_ref, before_mine_ref) if mine else (pack_other_ref, before_other_ref)
        for head in heads(half):
            col = half_cols(half, mine, head.start, HD)
            place = head if mine else slice(half + head.start, half + head.stop)
            if mine:
                state = keep_ref[head, :]
                grad = high_ref[head, :], low_ref[head, :]
            else:
                state = got_ref[sums_rows + head.start : sums_rows + head.stop, :]
                grad = gradient(factors, pack_ref, att_other_ref, head)
                query = split(pack_ref[head, :])
                total = None
            for n, row in reversed(list(enumerate(blocks(rows)))):
                part = steps(grad, row)
                if not mine and n > 0:
                    more = over_steps(part, steps(query, row))
                    total = more if total is None else total + more
                    after_ref[n - 1, head, :] = total
                part = [x.T for x in part]
                grad_high[row, place], grad_low[row, place] = part
                here = state_operand(state if n == 0 else state + before_ref[n - 1, head, :], True)
                gq_ref[row, col] = product_state(part, here, True)
    for mine in (True, False):
        for head in heads(half):
            col = half_cols(half, mine, head.start, HD)
            place = head if mine else slice(half + head.start, half + head.stop)
            for row in blocks(rows):
                grad = grad_high[row, place], grad_low[row, place]
                mixing = product_nt(grad, split(v_ref[row, col]))
                mixing = jnp.where(causal_mask(row.stop - row.start), mixing, 0.0)
                gq_ref[row, col] += product_nn(split(mixing), split(k_ref[row, col]))
                copies.append(pltpu.make_async_copy(gq_ref.at[row, col], gq_hbm.at[row, col], sems.at[len(copies)]))
                copies[-1].start()
    for mine in (True, False):
        pack_ref = pack_mine_ref if mine else pack_other_ref
        for head in heads(half):
            col = half_cols(half, mine, head.start, HD)
            place = head if mine else slice(half + head.start, half + head.stop)
            for row in blocks(rows):
                grad = grad_high[row, place], grad_low[row, place]
                query, key, value = split(pack_ref[head, row].T), split(k_ref[row, col]), split(v_ref[row, col])
                mask = causal_mask(row.stop - row.start, True)
                mixing = jnp.where(mask, product_nt(value, grad), 0.0)
                gk_ref[row, place] = product_nn(split(mixing), query)
                scores = jnp.where(mask, product_nt(key, query), 0.0)
                gv_ref[row, place] = product_nn(split(scores), grad)
    for copy in copies:
        copy.wait()


def grads_state(mine, k_ref, v_ref, gk_local_ref, gv_local_ref, state_ref, after_ref, *refs):
    gk_hbm, gv_hbm, gk_ref, gv_ref, sems = refs[-5:]
    rows, width = k_ref.shape
    half = width // 2
    last = len(blocks(rows)) - 1
    copies = []

    def leave(near, far, row, head, col):
        copies.append(pltpu.make_async_copy(near.at[row, head], far.at[row, col], sems.at[len(copies)]))
        copies[-1].start()

    for head in heads(half):
        col = half_cols(half, mine, head.start, HD)
        place = head if mine else slice(half + head.start, half + head.stop)
        for n, row in enumerate(blocks(rows)):
            here = state_ref[head, :] if n == last else state_ref[head, :] + after_ref[n, head, :]
            gk_ref[row, head] = gk_local_ref[row, place] + product_state(split(v_ref[row, col]), state_operand(here, False), False)
            leave(gk_ref, gk_hbm, row, head, col)
            gv_ref[row, head] = gv_local_ref[row, place] + product_state(split(k_ref[row, col]), state_operand(here, True), True)
            leave(gv_ref, gv_hbm, row, head, col)
    for copy in copies:
        copy.wait()


def swap(x, axis, distance):
    count = lax.axis_size(axis)
    return lax.ppermute(x, axis, [(i, i ^ distance) for i in range(count)])


def from_other_chips(pair, reverse):
    place = lax.axis_index("seq")
    chip = place // 2
    ahead = lambda d: (chip ^ d) > chip if reverse else (chip ^ d) < chip
    total = jnp.zeros_like(pair)
    if on_grid():
        got = [(d, swap(pair, "seq", 2 * d + d % 2)) for d in (3, 2, 1)]
        for d, part in got:
            total = total + jnp.where(ahead(d), part, 0.0)
        return total
    d = 1
    while d < lax.axis_size("seq") // 2:
        part = swap(pair, "seq", 2 * d)
        total = total + jnp.where(ahead(d), part, 0.0)
        pair = pair + part
        d *= 2
    return total


def sum_over_heads(x, same_x):
    count = lax.axis_size("head")
    if count > 4 or count & (count - 1):
        return lax.psum(same_x, "head")
    parts = []
    seqs = range(lax.axis_size("seq"))
    for d in reversed(range(1, count)):
        pairs = [(i * count + z, (i ^ 1) * count + (z ^ d)) for i in seqs for z in range(count)]
        parts.append(lax.ppermute(x, ("seq", "head"), pairs))
    for part in parts:
        same_x = same_x + part
    return same_x


def shards(queries, keys, values, cotangent, gain):
    rows, width = queries.shape
    full_width = width * lax.axis_size("head")
    half = width // 2
    count = len(blocks(rows))
    units = count * (width // HD)
    square = rows * width * HD * 2 * 3
    whole, halves, state = (rows, width), (rows, half), (half, HD)
    packed, across = (2 * half, rows), (half, rows)
    inner = (max(count - 1, 1), half, HD)
    first = lax.axis_index("seq") % 2 == 0
    gain = gain.reshape(1, width)

    other, before_other, near_keys, near_values, gain = call(
        key_states_other, "key_states_other", [state, inner, whole, whole, (1, width)], square // 2,
        [keys, values, gain], [pltpu.SemaphoreType.DMA((2, count)), pltpu.SemaphoreType.DMA], hbm_in=(0, 1, 2),
    )
    from_pair = swap(other, "seq", 1)
    mine, before_mine, pack_mine, pack_other = call(
        key_states_mine, "key_states_mine", [state, inner, packed, packed], square // 2,
        [near_keys, near_values, queries, cotangent, gain],
    )
    sibling = swap(pack_other, "seq", 1)
    earlier = from_other_chips(mine + from_pair, False)
    keep = earlier + jnp.where(first, 0.0, from_pair)
    give = earlier + jnp.where(first, mine, 0.0)
    local_mine, local_other = call(
        attend_local, "attend_local", [across, across], 5 * square,
        [pack_mine, pack_other, near_keys, near_values, before_mine, before_other],
    )
    sibling_local = swap(local_other, "seq", 1)
    attended, sibling_attended, sums = call(
        attend_state, "attend_state", [across, across, (4 * rows // LANES, LANES)], square,
        [pack_mine, local_mine, sibling, sibling_local, keep, give],
    )
    given = jnp.concatenate([sums, give], axis=0)
    got = swap(given, "seq", 1)
    pair_sums = given[: sums.shape[0]] + got[: sums.shape[0]]
    attended_other, same_pair_sums = call(
        attend_other, "attend_other", [across, sums.shape], square // 2, [pair_sums, got, pack_other, local_other]
    )
    sums = sum_over_heads(pair_sums, same_pair_sums)
    pair, own_grad, sibling_grad, after_mine, high, low = call(
        functools.partial(grad_states, full_width), "grad_states",
        [state, state, state, inner, (across, BF16), (across, BF16)], square,
        [sums, pack_mine, sibling, attended, sibling_attended],
    )
    later = from_other_chips(pair, True)
    grad_q, local_k, local_v, after_other, own_grad = call(
        functools.partial(grads_local, full_width), "grads_local", [whole, whole, whole, inner, state], 14 * square,
        [sums, got, high, low, attended_other, pack_mine, pack_other, keys, values, keep, before_mine, before_other, own_grad],
        [pltpu.VMEM(whole, F32), pltpu.VMEM(whole, BF16), pltpu.VMEM(whole, BF16), pltpu.SemaphoreType.DMA((units,))],
        hbm_out=(0,),
    )
    keep_later = later + jnp.where(first, sibling_grad, 0.0)
    got_later = swap(later + jnp.where(first, 0.0, own_grad), "seq", 1)
    scratch = [pltpu.VMEM(halves, F32), pltpu.VMEM(halves, F32), pltpu.SemaphoreType.DMA((units,))]
    grad_k, grad_v = call(
        functools.partial(grads_state, True), "grads_state_mine", [whole] * 2, square,
        [keys, values, local_k, local_v, keep_later, after_mine], scratch, hbm_out=(0, 1),
    )
    grad_k, grad_v = call(
        functools.partial(grads_state, False), "grads_state_other", [whole] * 2, square,
        [keys, values, local_k, local_v, got_later, after_other, grad_k, grad_v], scratch,
        hbm_in=(6, 7), hbm_out=(0, 1), aliases={6: 0, 7: 1},
    )
    return grad_q, grad_k, grad_v


def solution(mesh):
    in_specs = (P("seq", "head"), P("seq", "head"), P("seq", "head"), P("seq", "head"), P("head"))
    out_specs = (P("seq", "head"), P("seq", "head"), P("seq", "head"))
    return jax.shard_map(shards, mesh=mesh, in_specs=in_specs, out_specs=out_specs, check_vma=False)
```

```python
import functools
import jax
import jax.numpy as jnp
from jax import lax
from jax.experimental import pallas as pl
from jax.experimental.pallas import tpu as pltpu
from jax.sharding import PartitionSpec as P

HD = 128
BLOCK = 256
LANES = 128
F32 = jnp.float32
BF16 = jnp.bfloat16
NN = ((1,), (0,))
NT = ((1,), (1,))
TN = ((0,), (0,))


def split(x):
    high = x.astype(BF16)
    return high, (x - high.astype(F32)).astype(BF16)


def mul(left, right, dims):
    return lax.dot_general(left, right, (dims, ((), ())), preferred_element_type=F32)


def beside(*parts):
    return jnp.concatenate(parts, axis=1)


def product_nt(left, right):
    return mul(beside(*left), beside(right[0], right[0]), NT) + mul(left[0], right[1], NT)


def product_nn(left, right):
    size = right[0].shape[1]
    wide = mul(left[0], beside(*right), NN)
    return wide[:, :size] + wide[:, size:] + mul(left[1], right[0], NN)


def product_tn(left, right):
    rows, cols = left[0].shape[1], right[0].shape[1]
    wide = mul(beside(*left), beside(*right), TN)
    return wide[:rows, :cols] + wide[:rows, cols:] + wide[rows:, :cols]


def state_operand(state, transposed):
    high, low = split(state)
    if transposed:
        return jnp.concatenate([beside(high, high), beside(low, jnp.zeros_like(low))], axis=0)
    return jnp.concatenate([beside(high, low), beside(high, jnp.zeros_like(low))], axis=0)


def product_state(left, operand, transposed):
    wide = mul(beside(*left), operand, NT if transposed else NN)
    return wide[:, :HD] + wide[:, HD:]


def heads(width):
    return [slice(h * HD, (h + 1) * HD) for h in range(width // HD)]


def blocks(rows):
    size = min(BLOCK, rows)
    return [slice(n * size, (n + 1) * size) for n in range(rows // size)]


def call(body, name, outs, flops, operands, scratch=(), hbm_in=(), hbm_out=(), aliases=None):
    outs = [out if isinstance(out[0], tuple) else (out, F32) for out in outs]
    outs = [
        pltpu.HBM(*out) if i in hbm_out else jax.ShapeDtypeStruct(*out) for i, out in enumerate(outs)
    ]
    moved = 2 * sum(x.size * x.dtype.itemsize for x in operands)
    operands = [
        pltpu.with_memory_space_constraint(x, pltpu.HBM) if i in hbm_in else x for i, x in enumerate(operands)
    ]
    place = lambda far: pl.BlockSpec(memory_space=pltpu.HBM if far else pltpu.VMEM)
    return pl.pallas_call(
        body,
        out_shape=outs,
        in_specs=[place(i in hbm_in) for i in range(len(operands))],
        out_specs=[place(i in hbm_out) for i in range(len(outs))],
        scratch_shapes=list(scratch),
        input_output_aliases=aliases or {},
        name=name,
        cost_estimate=pl.CostEstimate(flops=flops, bytes_accessed=moved, transcendentals=0),
        compiler_params=pltpu.CompilerParams(vmem_limit_bytes=16 * 1024 * 1024),
    )(*operands)


def my_core():
    return lax.axis_index("seq") % 2


def on_grid():
    return lax.axis_size("seq") == 8


def my_half():
    place = lax.axis_index("seq")
    return (place + place // 2) % 2 if on_grid() else place % 2


def half_cols(half, mine, start=0, size=None):
    which = my_half() if mine else 1 - my_half()
    return pl.ds(pl.multiple_of(which * half + start, LANES), size or half)


def causal_mask(size, transposed=False):
    row = lax.broadcasted_iota(jnp.int32, (size, size), 0)
    col = lax.broadcasted_iota(jnp.int32, (size, size), 1)
    return row <= col if transposed else row >= col


def block_states(k_ref, v_ref, mine, total_ref, before_ref, ready=None):
    rows, width = k_ref.shape
    half = width // 2
    count = len(blocks(rows))
    for n, row in enumerate(blocks(rows)):
        if ready:
            ready(n)
        for head in heads(half):
            col = half_cols(half, mine, head.start, HD)
            state = product_tn(split(k_ref[row, col]), split(v_ref[row, col]))
            if n > 0:
                state = state + before_ref[n - 1, head, :]
            if n + 1 < count:
                before_ref[n, head, :] = state
            else:
                total_ref[head, :] = state


def key_states_other(k_hbm, v_hbm, gain_hbm, total_ref, before_ref, k_ref, v_ref, gain_ref, sems, gain_sem):
    gain_copy = pltpu.make_async_copy(gain_hbm, gain_ref, gain_sem)
    copies = []
    for n, row in enumerate(blocks(k_ref.shape[0])):
        copies.append([
            pltpu.make_async_copy(far.at[row], near.at[row], sems.at[i, n])
            for i, (far, near) in enumerate(((k_hbm, k_ref), (v_hbm, v_ref)))
        ])
        for copy in copies[n]:
            copy.start()
    gain_copy.start()

    def ready(n):
        for copy in copies[n]:
            copy.wait()

    block_states(k_ref, v_ref, False, total_ref, before_ref, ready)
    gain_copy.wait()


def key_states_mine(k_ref, v_ref, q_ref, cot_ref, gain_ref, total_ref, before_ref, mine_ref, other_ref):
    half = k_ref.shape[1] // 2
    block_states(k_ref, v_ref, True, total_ref, before_ref)
    for mine, pack_ref in ((True, mine_ref), (False, other_ref)):
        col = half_cols(half, mine)
        pack_ref[:half, :] = q_ref[:, col].T
        pack_ref[half:, :] = (gain_ref[:, col] * cot_ref[:, col]).T


def state_times(state, query):
    left = split(state.T)
    twice = jnp.concatenate([query[0], query[0]], axis=0)
    return mul(beside(*left), twice, NN) + mul(left[0], query[1], NN)


def over_steps(left, right):
    rows, cols = left[0].shape[0], right[0].shape[0]
    wide = mul(jnp.concatenate(left, axis=0), jnp.concatenate(right, axis=0), NT)
    return wide[:rows, :cols] + wide[:rows, cols:] + wide[rows:, :cols]


def attend_local(pack_mine_ref, pack_other_ref, k_ref, v_ref, before_mine_ref, before_other_ref, mine_ref, other_ref):
    rows, width = k_ref.shape
    half = width // 2
    parts = ((False, pack_other_ref, before_other_ref, other_ref), (True, pack_mine_ref, before_mine_ref, mine_ref))
    for mine, pack_ref, before_ref, out_ref in parts:
        for head in heads(half):
            col = half_cols(half, mine, head.start, HD)
            for n, row in enumerate(blocks(rows)):
                query = split(pack_ref[head, row])
                key = split(k_ref[row, col])
                twice = jnp.concatenate([query[0], query[0]], axis=0)
                scores = mul(beside(*key), twice, NN) + mul(key[0], query[1], NN)
                scores = split(jnp.where(causal_mask(scores.shape[0], True), scores, 0.0))
                value = split(v_ref[row, col].T)
                out = mul(value[0], scores[0], NN) + mul(value[0], scores[1], NN) + mul(value[1], scores[0], NN)
                if n > 0:
                    out = out + state_times(before_ref[n - 1, head, :], query)
                out_ref[head, row] = out


def lane_rows(x):
    return [x[:, start : start + LANES] for start in range(0, x.shape[1], LANES)]


def attend_state(own_ref, own_local_ref, sib_ref, sib_local_ref, keep_ref, give_ref, own_out_ref, sib_out_ref, sums_ref):
    half, rows = own_local_ref.shape
    count = rows // LANES
    for core, pack_ref, local_ref, state_ref, out_ref in (
        (my_core(), own_ref, own_local_ref, keep_ref, own_out_ref),
        (1 - my_core(), sib_ref, sib_local_ref, give_ref, sib_out_ref),
    ):
        squares, cross = jnp.zeros((1, rows), F32), jnp.zeros((1, rows), F32)
        for head in heads(half):
            out = local_ref[head, :] + state_times(state_ref[head, :], split(pack_ref[head, :]))
            out_ref[head, :] = out
            scaled = pack_ref[half + head.start : half + head.stop, :]
            squares = squares + jnp.sum(out * out, axis=0, keepdims=True)
            cross = cross + jnp.sum(scaled * out, axis=0, keepdims=True)
        place = pl.ds(pl.multiple_of(core * 2 * count, 2 * count), 2 * count)
        sums_ref[place, :] = jnp.concatenate(lane_rows(squares) + lane_rows(cross), axis=0)


def attend_other(pair_sums_ref, got_ref, pack_ref, local_ref, out_ref, same_sums_ref):
    same_sums_ref[...] = pair_sums_ref[...]
    start = pair_sums_ref.shape[0]
    for head in heads(local_ref.shape[0]):
        state = got_ref[start + head.start : start + head.stop, :]
        out_ref[head, :] = local_ref[head, :] + state_times(state, split(pack_ref[head, :]))


def step_factors(full_width, rows, sums_ref, own):
    count = rows // LANES
    core = my_core() if own else 1 - my_core()
    sums = sums_ref[pl.ds(pl.multiple_of(core * 2 * count, 2 * count), 2 * count), :]
    inverse = lax.rsqrt(sums[:count] / full_width + 1e-06)
    factor = inverse * inverse * inverse * (sums[count:] / full_width)
    return [beside(*[x[j : j + 1, :] for j in range(count)]) for x in (inverse, factor)]


def gradient(factors, pack_ref, att_ref, head):
    half = att_ref.shape[0]
    scaled = pack_ref[half + head.start : half + head.stop, :]
    return split(factors[0] * scaled - factors[1] * att_ref[head, :])


def steps(parts, row):
    return [part[:, row] for part in parts]


def grad_states(full_width, sums_ref, own_ref, sib_ref, own_att_ref, sib_att_ref, pair_ref, own_total_ref, sib_total_ref, after_ref, high_ref, low_ref):
    half, rows = own_att_ref.shape
    for own, pack_ref, att_ref, total_ref in ((False, sib_ref, sib_att_ref, sib_total_ref), (True, own_ref, own_att_ref, own_total_ref)):
        factors = step_factors(full_width, rows, sums_ref, own)
        for head in heads(half):
            grad = gradient(factors, pack_ref, att_ref, head)
            query = split(pack_ref[head, :])
            total = None
            for n, row in reversed(list(enumerate(blocks(rows)))):
                state = over_steps(steps(grad, row), steps(query, row))
                total = state if total is None else total + state
                if own and n > 0:
                    after_ref[n - 1, head, :] = total
            if own:
                high_ref[head, :], low_ref[head, :] = grad
            total_ref[head, :] = total
    pair_ref[...] = own_total_ref[...] + sib_total_ref[...]


def grads_local(full_width, sums_ref, got_ref, high_ref, low_ref, att_other_ref, pack_mine_ref, pack_other_ref, k_ref, v_ref, keep_ref, before_mine_ref, before_other_ref, total_ref, gq_hbm, gk_ref, gv_ref, after_ref, same_total_ref, gq_ref, grad_high, grad_low, sems):
    rows, width = k_ref.shape
    half = width // 2
    sums_rows = 4 * rows // LANES
    same_total_ref[...] = total_ref[...]
    factors = step_factors(full_width, rows, sums_ref, True)
    copies = []
    for mine in (True, False):
        pack_ref, before_ref = (pack_mine_ref, before_mine_ref) if mine else (pack_other_ref, before_other_ref)
        for head in heads(half):
            col = half_cols(half, mine, head.start, HD)
            place = head if mine else slice(half + head.start, half + head.stop)
            if mine:
                state = keep_ref[head, :]
                grad = high_ref[head, :], low_ref[head, :]
            else:
                state = got_ref[sums_rows + head.start : sums_rows + head.stop, :]
                grad = gradient(factors, pack_ref, att_other_ref, head)
                query = split(pack_ref[head, :])
                total = None
            for n, row in reversed(list(enumerate(blocks(rows)))):
                part = steps(grad, row)
                if not mine and n > 0:
                    more = over_steps(part, steps(query, row))
                    total = more if total is None else total + more
                    after_ref[n - 1, head, :] = total
                part = [x.T for x in part]
                grad_high[row, place], grad_low[row, place] = part
                here = state_operand(state if n == 0 else state + before_ref[n - 1, head, :], True)
                gq_ref[row, col] = product_state(part, here, True)
    for mine in (True, False):
        for head in heads(half):
            col = half_cols(half, mine, head.start, HD)
            place = head if mine else slice(half + head.start, half + head.stop)
            for row in blocks(rows):
                grad = grad_high[row, place], grad_low[row, place]
                mixing = product_nt(grad, split(v_ref[row, col]))
                mixing = jnp.where(causal_mask(row.stop - row.start), mixing, 0.0)
                gq_ref[row, col] += product_nn(split(mixing), split(k_ref[row, col]))
                copies.append(pltpu.make_async_copy(gq_ref.at[row, col], gq_hbm.at[row, col], sems.at[len(copies)]))
                copies[-1].start()
    for mine in (True, False):
        pack_ref = pack_mine_ref if mine else pack_other_ref
        for head in heads(half):
            col = half_cols(half, mine, head.start, HD)
            place = head if mine else slice(half + head.start, half + head.stop)
            for row in blocks(rows):
                grad = grad_high[row, place], grad_low[row, place]
                query, key, value = split(pack_ref[head, row].T), split(k_ref[row, col]), split(v_ref[row, col])
                mask = causal_mask(row.stop - row.start, True)
                mixing = jnp.where(mask, product_nt(value, grad), 0.0)
                gk_ref[row, place] = product_nn(split(mixing), query)
                scores = jnp.where(mask, product_nt(key, query), 0.0)
                gv_ref[row, place] = product_nn(split(scores), grad)
    for copy in copies:
        copy.wait()


def grads_state(mine, k_ref, v_ref, gk_local_ref, gv_local_ref, state_ref, after_ref, *refs):
    gk_hbm, gv_hbm, gk_ref, gv_ref, sems = refs[-5:]
    rows, width = k_ref.shape
    half = width // 2
    last = len(blocks(rows)) - 1
    copies = []

    def leave(near, far, row, head, col):
        copies.append(pltpu.make_async_copy(near.at[row, head], far.at[row, col], sems.at[len(copies)]))
        copies[-1].start()

    for head in heads(half):
        col = half_cols(half, mine, head.start, HD)
        place = head if mine else slice(half + head.start, half + head.stop)
        for n, row in enumerate(blocks(rows)):
            here = state_ref[head, :] if n == last else state_ref[head, :] + after_ref[n, head, :]
            gk_ref[row, head] = gk_local_ref[row, place] + product_state(split(v_ref[row, col]), state_operand(here, False), False)
            leave(gk_ref, gk_hbm, row, head, col)
            gv_ref[row, head] = gv_local_ref[row, place] + product_state(split(k_ref[row, col]), state_operand(here, True), True)
            leave(gv_ref, gv_hbm, row, head, col)
    for copy in copies:
        copy.wait()


def swap(x, axis, distance):
    count = lax.axis_size(axis)
    return lax.ppermute(x, axis, [(i, i ^ distance) for i in range(count)])


def from_other_chips(pair, reverse):
    place = lax.axis_index("seq")
    chip = place // 2
    ahead = lambda d: (chip ^ d) > chip if reverse else (chip ^ d) < chip
    total = jnp.zeros_like(pair)
    if on_grid():
        got = [(d, swap(pair, "seq", 2 * d + d % 2)) for d in (3, 1, 2)]
        for d, part in got:
            total = total + jnp.where(ahead(d), part, 0.0)
        return total
    d = 1
    while d < lax.axis_size("seq") // 2:
        part = swap(pair, "seq", 2 * d)
        total = total + jnp.where(ahead(d), part, 0.0)
        pair = pair + part
        d *= 2
    return total


def sum_over_heads(x, same_x):
    count = lax.axis_size("head")
    if count > 4 or count & (count - 1):
        return lax.psum(same_x, "head")
    parts = []
    seqs = range(lax.axis_size("seq"))
    for d in sorted(range(1, count), key=lambda d: (d != count // 2, -d)):
        pairs = [(i * count + z, (i ^ 1) * count + (z ^ d)) for i in seqs for z in range(count)]
        parts.append(lax.ppermute(x, ("seq", "head"), pairs))
    for part in parts:
        same_x = same_x + part
    return same_x


def shards(queries, keys, values, cotangent, gain):
    rows, width = queries.shape
    full_width = width * lax.axis_size("head")
    half = width // 2
    count = len(blocks(rows))
    units = count * (width // HD)
    square = rows * width * HD * 2 * 3
    whole, halves, state = (rows, width), (rows, half), (half, HD)
    packed, across = (2 * half, rows), (half, rows)
    inner = (max(count - 1, 1), half, HD)
    first = lax.axis_index("seq") % 2 == 0
    gain = gain.reshape(1, width)

    other, before_other, near_keys, near_values, gain = call(
        key_states_other, "key_states_other", [state, inner, whole, whole, (1, width)], square // 2,
        [keys, values, gain], [pltpu.SemaphoreType.DMA((2, count)), pltpu.SemaphoreType.DMA], hbm_in=(0, 1, 2),
    )
    from_pair = swap(other, "seq", 1)
    mine, before_mine, pack_mine, pack_other = call(
        key_states_mine, "key_states_mine", [state, inner, packed, packed], square // 2,
        [near_keys, near_values, queries, cotangent, gain],
    )
    sibling = swap(pack_other, "seq", 1)
    earlier = from_other_chips(mine + from_pair, False)
    keep = earlier + jnp.where(first, 0.0, from_pair)
    give = earlier + jnp.where(first, mine, 0.0)
    local_mine, local_other = call(
        attend_local, "attend_local", [across, across], 5 * square,
        [pack_mine, pack_other, near_keys, near_values, before_mine, before_other],
    )
    sibling_local = swap(local_other, "seq", 1)
    attended, sibling_attended, sums = call(
        attend_state, "attend_state", [across, across, (4 * rows // LANES, LANES)], square,
        [pack_mine, local_mine, sibling, sibling_local, keep, give],
    )
    given = jnp.concatenate([sums, give], axis=0)
    got = swap(given, "seq", 1)
    pair_sums = given[: sums.shape[0]] + got[: sums.shape[0]]
    attended_other, same_pair_sums = call(
        attend_other, "attend_other", [across, sums.shape], square // 2, [pair_sums, got, pack_other, local_other]
    )
    sums = sum_over_heads(pair_sums, same_pair_sums)
    pair, own_grad, sibling_grad, after_mine, high, low = call(
        functools.partial(grad_states, full_width), "grad_states",
        [state, state, state, inner, (across, BF16), (across, BF16)], square,
        [sums, pack_mine, sibling, attended, sibling_attended],
    )
    later = from_other_chips(pair, True)
    grad_q, local_k, local_v, after_other, own_grad = call(
        functools.partial(grads_local, full_width), "grads_local", [whole, whole, whole, inner, state], 14 * square,
        [sums, got, high, low, attended_other, pack_mine, pack_other, keys, values, keep, before_mine, before_other, own_grad],
        [pltpu.VMEM(whole, F32), pltpu.VMEM(whole, BF16), pltpu.VMEM(whole, BF16), pltpu.SemaphoreType.DMA((units,))],
        hbm_out=(0,),
    )
    keep_later = later + jnp.where(first, sibling_grad, 0.0)
    got_later = swap(later + jnp.where(first, 0.0, own_grad), "seq", 1)
    scratch = [pltpu.VMEM(halves, F32), pltpu.VMEM(halves, F32), pltpu.SemaphoreType.DMA((units,))]
    grad_k, grad_v = call(
        functools.partial(grads_state, True), "grads_state_mine", [whole] * 2, square,
        [keys, values, local_k, local_v, keep_later, after_mine], scratch, hbm_out=(0, 1),
    )
    grad_k, grad_v = call(
        functools.partial(grads_state, False), "grads_state_other", [whole] * 2, square,
        [keys, values, local_k, local_v, got_later, after_other, grad_k, grad_v], scratch,
        hbm_in=(6, 7), hbm_out=(0, 1), aliases={6: 0, 7: 1},
    )
    return grad_q, grad_k, grad_v


def solution(mesh):
    in_specs = (P("seq", "head"), P("seq", "head"), P("seq", "head"), P("seq", "head"), P("head"))
    out_specs = (P("seq", "head"), P("seq", "head"), P("seq", "head"))
    return jax.shard_map(shards, mesh=mesh, in_specs=in_specs, out_specs=out_specs, check_vma=False)
```

```python
import functools
import jax
import jax.numpy as jnp
from jax import lax
from jax.experimental import pallas as pl
from jax.experimental.pallas import tpu as pltpu
from jax.sharding import PartitionSpec as P

HD = 128
BLOCK = 256
LANES = 128
F32 = jnp.float32
BF16 = jnp.bfloat16
NN = ((1,), (0,))
NT = ((1,), (1,))
TN = ((0,), (0,))


def split(x):
    high = x.astype(BF16)
    return high, (x - high.astype(F32)).astype(BF16)


def mul(left, right, dims):
    return lax.dot_general(left, right, (dims, ((), ())), preferred_element_type=F32)


def beside(*parts):
    return jnp.concatenate(parts, axis=1)


def product_nt(left, right):
    return mul(beside(*left), beside(right[0], right[0]), NT) + mul(left[0], right[1], NT)


def product_nn(left, right):
    size = right[0].shape[1]
    wide = mul(left[0], beside(*right), NN)
    return wide[:, :size] + wide[:, size:] + mul(left[1], right[0], NN)


def product_tn(left, right):
    rows, cols = left[0].shape[1], right[0].shape[1]
    wide = mul(beside(*left), beside(*right), TN)
    return wide[:rows, :cols] + wide[:rows, cols:] + wide[rows:, :cols]


def state_operand(state, transposed):
    high, low = split(state)
    if transposed:
        return jnp.concatenate([beside(high, high), beside(low, jnp.zeros_like(low))], axis=0)
    return jnp.concatenate([beside(high, low), beside(high, jnp.zeros_like(low))], axis=0)


def product_parts(left, operand, transposed):
    wide = mul(left, operand, NT if transposed else NN)
    return wide[:, :HD] + wide[:, HD:]


def product_state(left, operand, transposed):
    wide = mul(beside(*left), operand, NT if transposed else NN)
    return wide[:, :HD] + wide[:, HD:]


def heads(width):
    return [slice(h * HD, (h + 1) * HD) for h in range(width // HD)]


def blocks(rows):
    size = min(BLOCK, rows)
    return [slice(n * size, (n + 1) * size) for n in range(rows // size)]


def call(body, name, outs, flops, operands, scratch=(), hbm_in=(), hbm_out=(), aliases=None):
    outs = [out if isinstance(out[0], tuple) else (out, F32) for out in outs]
    outs = [
        pltpu.HBM(*out) if i in hbm_out else jax.ShapeDtypeStruct(*out) for i, out in enumerate(outs)
    ]
    moved = 2 * sum(x.size * x.dtype.itemsize for x in operands)
    operands = [
        pltpu.with_memory_space_constraint(x, pltpu.HBM) if i in hbm_in else x for i, x in enumerate(operands)
    ]
    place = lambda far: pl.BlockSpec(memory_space=pltpu.HBM if far else pltpu.VMEM)
    return pl.pallas_call(
        body,
        out_shape=outs,
        in_specs=[place(i in hbm_in) for i in range(len(operands))],
        out_specs=[place(i in hbm_out) for i in range(len(outs))],
        scratch_shapes=list(scratch),
        input_output_aliases=aliases or {},
        name=name,
        cost_estimate=pl.CostEstimate(flops=flops, bytes_accessed=moved, transcendentals=0),
        compiler_params=pltpu.CompilerParams(vmem_limit_bytes=16 * 1024 * 1024),
    )(*operands)


def my_core():
    return lax.axis_index("seq") % 2


def on_grid():
    return lax.axis_size("seq") == 8


def my_half():
    place = lax.axis_index("seq")
    return (place + place // 2) % 2 if on_grid() else place % 2


def half_cols(half, mine, start=0, size=None):
    which = my_half() if mine else 1 - my_half()
    return pl.ds(pl.multiple_of(which * half + start, LANES), size or half)


def causal_mask(size, transposed=False):
    row = lax.broadcasted_iota(jnp.int32, (size, size), 0)
    col = lax.broadcasted_iota(jnp.int32, (size, size), 1)
    return row <= col if transposed else row >= col


def block_states(k_ref, v_ref, mine, total_ref, before_ref, ready=None):
    rows, width = k_ref.shape
    half = width // 2
    count = len(blocks(rows))
    for n, row in enumerate(blocks(rows)):
        if ready:
            ready(n)
        for head in heads(half):
            col = half_cols(half, mine, head.start, HD)
            state = product_tn(split(k_ref[row, col]), split(v_ref[row, col]))
            if n > 0:
                state = state + before_ref[n - 1, head, :]
            if n + 1 < count:
                before_ref[n, head, :] = state
            else:
                total_ref[head, :] = state


def key_states_other(k_hbm, v_hbm, gain_hbm, total_ref, before_ref, k_ref, v_ref, gain_ref, sems, gain_sem):
    gain_copy = pltpu.make_async_copy(gain_hbm, gain_ref, gain_sem)
    copies = []
    for n, row in enumerate(blocks(k_ref.shape[0])):
        copies.append([
            pltpu.make_async_copy(far.at[row], near.at[row], sems.at[i, n])
            for i, (far, near) in enumerate(((k_hbm, k_ref), (v_hbm, v_ref)))
        ])
        for copy in copies[n]:
            copy.start()
    gain_copy.start()

    def ready(n):
        for copy in copies[n]:
            copy.wait()

    block_states(k_ref, v_ref, False, total_ref, before_ref, ready)
    gain_copy.wait()


def key_states_mine(k_ref, v_ref, q_ref, cot_ref, gain_ref, total_ref, before_ref, mine_ref, other_ref):
    half = k_ref.shape[1] // 2
    block_states(k_ref, v_ref, True, total_ref, before_ref)
    for mine, pack_ref in ((True, mine_ref), (False, other_ref)):
        col = half_cols(half, mine)
        pack_ref[:half, :] = q_ref[:, col].T
        pack_ref[half:, :] = (gain_ref[:, col] * cot_ref[:, col]).T


def state_times(state, query):
    left = split(state.T)
    twice = jnp.concatenate([query[0], query[0]], axis=0)
    return mul(beside(*left), twice, NN) + mul(left[0], query[1], NN)


def over_steps(left, right):
    rows, cols = left[0].shape[0], right[0].shape[0]
    wide = mul(jnp.concatenate(left, axis=0), jnp.concatenate(right, axis=0), NT)
    return wide[:rows, :cols] + wide[:rows, cols:] + wide[rows:, :cols]


def attend_local(pack_mine_ref, pack_other_ref, k_ref, v_ref, before_mine_ref, before_other_ref, mine_ref, other_ref):
    rows, width = k_ref.shape
    half = width // 2
    parts = ((False, pack_other_ref, before_other_ref, other_ref), (True, pack_mine_ref, before_mine_ref, mine_ref))
    for mine, pack_ref, before_ref, out_ref in parts:
        for head in heads(half):
            col = half_cols(half, mine, head.start, HD)
            for n, row in enumerate(blocks(rows)):
                query = split(pack_ref[head, row])
                key = split(k_ref[row, col])
                twice = jnp.concatenate([query[0], query[0]], axis=0)
                scores = mul(beside(*key), twice, NN) + mul(key[0], query[1], NN)
                scores = split(jnp.where(causal_mask(scores.shape[0], True), scores, 0.0))
                value = split(v_ref[row, col].T)
                out = mul(value[0], scores[0], NN) + mul(value[0], scores[1], NN) + mul(value[1], scores[0], NN)
                if n > 0:
                    out = out + state_times(before_ref[n - 1, head, :], query)
                out_ref[head, row] = out


def lane_rows(x):
    return [x[:, start : start + LANES] for start in range(0, x.shape[1], LANES)]


def attend_state(own_ref, own_local_ref, sib_ref, sib_local_ref, keep_ref, give_ref, own_out_ref, sib_out_ref, sums_ref):
    half, rows = own_local_ref.shape
    count = rows // LANES
    for core, pack_ref, local_ref, state_ref, out_ref in (
        (my_core(), own_ref, own_local_ref, keep_ref, own_out_ref),
        (1 - my_core(), sib_ref, sib_local_ref, give_ref, sib_out_ref),
    ):
        squares, cross = jnp.zeros((1, rows), F32), jnp.zeros((1, rows), F32)
        for head in heads(half):
            out = local_ref[head, :] + state_times(state_ref[head, :], split(pack_ref[head, :]))
            out_ref[head, :] = out
            scaled = pack_ref[half + head.start : half + head.stop, :]
            squares = squares + jnp.sum(out * out, axis=0, keepdims=True)
            cross = cross + jnp.sum(scaled * out, axis=0, keepdims=True)
        place = pl.ds(pl.multiple_of(core * 2 * count, 2 * count), 2 * count)
        sums_ref[place, :] = jnp.concatenate(lane_rows(squares) + lane_rows(cross), axis=0)


def attend_other(pair_sums_ref, got_ref, pack_ref, local_ref, out_ref, same_sums_ref):
    same_sums_ref[...] = pair_sums_ref[...]
    start = pair_sums_ref.shape[0]
    for head in heads(local_ref.shape[0]):
        state = got_ref[start + head.start : start + head.stop, :]
        out_ref[head, :] = local_ref[head, :] + state_times(state, split(pack_ref[head, :]))


def step_factors(full_width, rows, sums_ref, own):
    count = rows // LANES
    core = my_core() if own else 1 - my_core()
    sums = sums_ref[pl.ds(pl.multiple_of(core * 2 * count, 2 * count), 2 * count), :]
    inverse = lax.rsqrt(sums[:count] / full_width + 1e-06)
    factor = inverse * inverse * inverse * (sums[count:] / full_width)
    return [beside(*[x[j : j + 1, :] for j in range(count)]) for x in (inverse, factor)]


def gradient(factors, pack_ref, att_ref, head):
    half = att_ref.shape[0]
    scaled = pack_ref[half + head.start : half + head.stop, :]
    return split(factors[0] * scaled - factors[1] * att_ref[head, :])


def steps(parts, row):
    return [part[:, row] for part in parts]


def grad_states(full_width, sums_ref, own_ref, sib_ref, own_att_ref, sib_att_ref, pair_ref, own_total_ref, sib_total_ref, after_ref, high_ref, low_ref):
    half, rows = own_att_ref.shape
    for own, pack_ref, att_ref, total_ref in ((False, sib_ref, sib_att_ref, sib_total_ref), (True, own_ref, own_att_ref, own_total_ref)):
        factors = step_factors(full_width, rows, sums_ref, own)
        for head in heads(half):
            grad = gradient(factors, pack_ref, att_ref, head)
            query = split(pack_ref[head, :])
            total = None
            for n, row in reversed(list(enumerate(blocks(rows)))):
                state = over_steps(steps(grad, row), steps(query, row))
                total = state if total is None else total + state
                if own and n > 0:
                    after_ref[n - 1, head, :] = total
            if own:
                high_ref[head, :], low_ref[head, :] = grad
            total_ref[head, :] = total
    pair_ref[...] = own_total_ref[...] + sib_total_ref[...]


def grads_local(full_width, sums_ref, got_ref, high_ref, low_ref, att_other_ref, pack_mine_ref, pack_other_ref, k_ref, v_ref, keep_ref, before_mine_ref, before_other_ref, total_ref, gq_hbm, gk_ref, gv_ref, after_ref, same_total_ref, k_parts_ref, v_parts_ref, gq_ref, grad_high, grad_low, sems):
    rows, width = k_ref.shape
    half = width // 2
    sums_rows = 4 * rows // LANES
    same_total_ref[...] = total_ref[...]
    factors = step_factors(full_width, rows, sums_ref, True)
    copies = []
    for mine in (True, False):
        pack_ref, before_ref = (pack_mine_ref, before_mine_ref) if mine else (pack_other_ref, before_other_ref)
        for head in heads(half):
            col = half_cols(half, mine, head.start, HD)
            place = head if mine else slice(half + head.start, half + head.stop)
            if mine:
                state = keep_ref[head, :]
                grad = high_ref[head, :], low_ref[head, :]
            else:
                state = got_ref[sums_rows + head.start : sums_rows + head.stop, :]
                grad = gradient(factors, pack_ref, att_other_ref, head)
                query = split(pack_ref[head, :])
                total = None
            for n, row in reversed(list(enumerate(blocks(rows)))):
                part = steps(grad, row)
                if not mine and n > 0:
                    more = over_steps(part, steps(query, row))
                    total = more if total is None else total + more
                    after_ref[n - 1, head, :] = total
                part = [x.T for x in part]
                grad_high[row, place], grad_low[row, place] = part
                here = state_operand(state if n == 0 else state + before_ref[n - 1, head, :], True)
                gq_ref[row, col] = product_state(part, here, True)
    for mine in (True, False):
        for head in heads(half):
            col = half_cols(half, mine, head.start, HD)
            place = head if mine else slice(half + head.start, half + head.stop)
            for row in blocks(rows):
                grad = grad_high[row, place], grad_low[row, place]
                mixing = product_nt(grad, split(v_ref[row, col]))
                mixing = jnp.where(causal_mask(row.stop - row.start), mixing, 0.0)
                gq_ref[row, col] += product_nn(split(mixing), split(k_ref[row, col]))
                copies.append(pltpu.make_async_copy(gq_ref.at[row, col], gq_hbm.at[row, col], sems.at[len(copies)]))
                copies[-1].start()
    for mine in (True, False):
        pack_ref = pack_mine_ref if mine else pack_other_ref
        for head in heads(half):
            col = half_cols(half, mine, head.start, HD)
            place = head if mine else slice(half + head.start, half + head.stop)
            for row in blocks(rows):
                grad = grad_high[row, place], grad_low[row, place]
                query, key, value = split(pack_ref[head, row].T), split(k_ref[row, col]), split(v_ref[row, col])
                parts = slice(2 * place.start, 2 * place.stop)
                k_parts_ref[row, parts], v_parts_ref[row, parts] = beside(*key), beside(*value)
                mask = causal_mask(row.stop - row.start, True)
                mixing = jnp.where(mask, product_nt(value, grad), 0.0)
                gk_ref[row, place] = product_nn(split(mixing), query)
                scores = jnp.where(mask, product_nt(key, query), 0.0)
                gv_ref[row, place] = product_nn(split(scores), grad)
    for copy in copies:
        copy.wait()


def grads_state(mine, k_ref, v_ref, gk_local_ref, gv_local_ref, state_ref, after_ref, *refs):
    gk_hbm, gv_hbm, gk_ref, gv_ref, sems = refs[-5:]
    rows, width = gk_local_ref.shape
    half = width // 2
    last = len(blocks(rows)) - 1
    copies = []

    def leave(near, far, row, head, col):
        copies.append(pltpu.make_async_copy(near.at[row, head], far.at[row, col], sems.at[len(copies)]))
        copies[-1].start()

    for head in heads(half):
        col = half_cols(half, mine, head.start, HD)
        place = head if mine else slice(half + head.start, half + head.stop)
        parts = slice(2 * place.start, 2 * place.stop)
        for n, row in enumerate(blocks(rows)):
            here = state_ref[head, :] if n == last else state_ref[head, :] + after_ref[n, head, :]
            gk_ref[row, head] = gk_local_ref[row, place] + product_parts(v_ref[row, parts], state_operand(here, False), False)
            leave(gk_ref, gk_hbm, row, head, col)
            gv_ref[row, head] = gv_local_ref[row, place] + product_parts(k_ref[row, parts], state_operand(here, True), True)
            leave(gv_ref, gv_hbm, row, head, col)
    for copy in copies:
        copy.wait()


def swap(x, axis, distance):
    count = lax.axis_size(axis)
    return lax.ppermute(x, axis, [(i, i ^ distance) for i in range(count)])


def from_other_chips(pair, reverse):
    place = lax.axis_index("seq")
    chip = place // 2
    ahead = lambda d: (chip ^ d) > chip if reverse else (chip ^ d) < chip
    total = jnp.zeros_like(pair)
    if on_grid():
        got = [(d, swap(pair, "seq", 2 * d + d % 2)) for d in (2, 1, 3)]
        for d, part in got:
            total = total + jnp.where(ahead(d), part, 0.0)
        return total
    d = 1
    while d < lax.axis_size("seq") // 2:
        part = swap(pair, "seq", 2 * d)
        total = total + jnp.where(ahead(d), part, 0.0)
        pair = pair + part
        d *= 2
    return total


def sum_over_heads(x, same_x):
    count = lax.axis_size("head")
    if count > 4 or count & (count - 1):
        return lax.psum(same_x, "head")
    parts = []
    seqs = range(lax.axis_size("seq"))
    for d in sorted(range(1, count), key=lambda d: (d == count // 2, d)):
        pairs = [(i * count + z, (i ^ 1) * count + (z ^ d)) for i in seqs for z in range(count)]
        parts.append(lax.ppermute(x, ("seq", "head"), pairs))
    for part in parts:
        same_x = same_x + part
    return same_x


def shards(queries, keys, values, cotangent, gain):
    rows, width = queries.shape
    full_width = width * lax.axis_size("head")
    half = width // 2
    count = len(blocks(rows))
    units = count * (width // HD)
    square = rows * width * HD * 2 * 3
    whole, halves, state = (rows, width), (rows, half), (half, HD)
    packed, across = (2 * half, rows), (half, rows)
    inner = (max(count - 1, 1), half, HD)
    first = lax.axis_index("seq") % 2 == 0
    gain = gain.reshape(1, width)

    other, before_other, near_keys, near_values, gain = call(
        key_states_other, "key_states_other", [state, inner, whole, whole, (1, width)], square // 2,
        [keys, values, gain], [pltpu.SemaphoreType.DMA((2, count)), pltpu.SemaphoreType.DMA], hbm_in=(0, 1, 2),
    )
    from_pair = swap(other, "seq", 1)
    mine, before_mine, pack_mine, pack_other = call(
        key_states_mine, "key_states_mine", [state, inner, packed, packed], square // 2,
        [near_keys, near_values, queries, cotangent, gain],
    )
    sibling = swap(pack_other, "seq", 1)
    earlier = from_other_chips(mine + from_pair, False)
    keep = earlier + jnp.where(first, 0.0, from_pair)
    give = earlier + jnp.where(first, mine, 0.0)
    local_mine, local_other = call(
        attend_local, "attend_local", [across, across], 5 * square,
        [pack_mine, pack_other, near_keys, near_values, before_mine, before_other],
    )
    sibling_local = swap(local_other, "seq", 1)
    attended, sibling_attended, sums = call(
        attend_state, "attend_state", [across, across, (4 * rows // LANES, LANES)], square,
        [pack_mine, local_mine, sibling, sibling_local, keep, give],
    )
    given = jnp.concatenate([sums, give], axis=0)
    got = swap(given, "seq", 1)
    pair_sums = given[: sums.shape[0]] + got[: sums.shape[0]]
    attended_other, same_pair_sums = call(
        attend_other, "attend_other", [across, sums.shape], square // 2, [pair_sums, got, pack_other, local_other]
    )
    sums = sum_over_heads(pair_sums, same_pair_sums)
    pair, own_grad, sibling_grad, after_mine, high, low = call(
        functools.partial(grad_states, full_width), "grad_states",
        [state, state, state, inner, (across, BF16), (across, BF16)], square,
        [sums, pack_mine, sibling, attended, sibling_attended],
    )
    later = from_other_chips(pair, True)
    grad_q, local_k, local_v, after_other, own_grad, key_parts, value_parts = call(
        functools.partial(grads_local, full_width), "grads_local",
        [whole, whole, whole, inner, state, ((rows, 2 * width), BF16), ((rows, 2 * width), BF16)], 14 * square,
        [sums, got, high, low, attended_other, pack_mine, pack_other, keys, values, keep, before_mine, before_other, own_grad],
        [pltpu.VMEM(whole, F32), pltpu.VMEM(whole, BF16), pltpu.VMEM(whole, BF16), pltpu.SemaphoreType.DMA((units,))],
        hbm_out=(0,),
    )
    keep_later = later + jnp.where(first, sibling_grad, 0.0)
    got_later = swap(later + jnp.where(first, 0.0, own_grad), "seq", 1)
    scratch = [pltpu.VMEM(halves, F32), pltpu.VMEM(halves, F32), pltpu.SemaphoreType.DMA((units,))]
    grad_k, grad_v = call(
        functools.partial(grads_state, True), "grads_state_mine", [whole] * 2, square,
        [key_parts, value_parts, local_k, local_v, keep_later, after_mine], scratch, hbm_out=(0, 1),
    )
    grad_k, grad_v = call(
        functools.partial(grads_state, False), "grads_state_other", [whole] * 2, square,
        [key_parts, value_parts, local_k, local_v, got_later, after_other, grad_k, grad_v], scratch,
        hbm_in=(6, 7), hbm_out=(0, 1), aliases={6: 0, 7: 1},
    )
    return grad_q, grad_k, grad_v


def solution(mesh):
    in_specs = (P("seq", "head"), P("seq", "head"), P("seq", "head"), P("seq", "head"), P("head"))
    out_specs = (P("seq", "head"), P("seq", "head"), P("seq", "head"))
    return jax.shard_map(shards, mesh=mesh, in_specs=in_specs, out_specs=out_specs, check_vma=False)
```

```python
import functools
import jax
import jax.numpy as jnp
from jax import lax
from jax.experimental import pallas as pl
from jax.experimental.pallas import tpu as pltpu
from jax.sharding import PartitionSpec as P

HD = 128
BLOCK = 256
LANES = 128
F32 = jnp.float32
BF16 = jnp.bfloat16
NN = ((1,), (0,))
NT = ((1,), (1,))
TN = ((0,), (0,))


def split(x):
    high = x.astype(BF16)
    return high, (x - high.astype(F32)).astype(BF16)


def mul(left, right, dims):
    return lax.dot_general(left, right, (dims, ((), ())), preferred_element_type=F32)


def beside(*parts):
    return jnp.concatenate(parts, axis=1)


def product_nt(left, right):
    return mul(beside(*left), beside(right[0], right[0]), NT) + mul(left[0], right[1], NT)


def product_nn(left, right):
    size = right[0].shape[1]
    wide = mul(left[0], beside(*right), NN)
    return wide[:, :size] + wide[:, size:] + mul(left[1], right[0], NN)


def product_tn(left, right):
    rows, cols = left[0].shape[1], right[0].shape[1]
    wide = mul(beside(*left), beside(*right), TN)
    return wide[:rows, :cols] + wide[:rows, cols:] + wide[rows:, :cols]


def state_operand(state, transposed):
    high, low = split(state)
    if transposed:
        return jnp.concatenate([beside(high, high), beside(low, jnp.zeros_like(low))], axis=0)
    return jnp.concatenate([beside(high, low), beside(high, jnp.zeros_like(low))], axis=0)


def product_state(left, operand, transposed):
    wide = mul(beside(*left), operand, NT if transposed else NN)
    return wide[:, :HD] + wide[:, HD:]


def heads(width):
    return [slice(h * HD, (h + 1) * HD) for h in range(width // HD)]


def blocks(rows):
    size = min(BLOCK, rows)
    return [slice(n * size, (n + 1) * size) for n in range(rows // size)]


def call(body, name, outs, flops, operands, scratch=(), hbm_in=(), hbm_out=(), aliases=None):
    outs = [out if isinstance(out[0], tuple) else (out, F32) for out in outs]
    outs = [
        pltpu.HBM(*out) if i in hbm_out else jax.ShapeDtypeStruct(*out) for i, out in enumerate(outs)
    ]
    moved = 2 * sum(x.size * x.dtype.itemsize for x in operands)
    operands = [
        pltpu.with_memory_space_constraint(x, pltpu.HBM) if i in hbm_in else x for i, x in enumerate(operands)
    ]
    place = lambda far: pl.BlockSpec(memory_space=pltpu.HBM if far else pltpu.VMEM)
    return pl.pallas_call(
        body,
        out_shape=outs,
        in_specs=[place(i in hbm_in) for i in range(len(operands))],
        out_specs=[place(i in hbm_out) for i in range(len(outs))],
        scratch_shapes=list(scratch),
        input_output_aliases=aliases or {},
        name=name,
        cost_estimate=pl.CostEstimate(flops=flops, bytes_accessed=moved, transcendentals=0),
        compiler_params=pltpu.CompilerParams(vmem_limit_bytes=16 * 1024 * 1024),
    )(*operands)


def my_core():
    return lax.axis_index("seq") % 2


def on_grid():
    return lax.axis_size("seq") == 8


def my_half():
    place = lax.axis_index("seq")
    return (place + place // 2) % 2 if on_grid() else place % 2


def half_cols(half, mine, start=0, size=None):
    which = my_half() if mine else 1 - my_half()
    return pl.ds(pl.multiple_of(which * half + start, LANES), size or half)


def causal_mask(size, transposed=False):
    row = lax.broadcasted_iota(jnp.int32, (size, size), 0)
    col = lax.broadcasted_iota(jnp.int32, (size, size), 1)
    return row <= col if transposed else row >= col


def block_states(k_ref, v_ref, mine, total_ref, before_ref, ready=None):
    rows, width = k_ref.shape
    half = width // 2
    count = len(blocks(rows))
    for n, row in enumerate(blocks(rows)):
        if ready:
            ready(n)
        for head in heads(half):
            col = half_cols(half, mine, head.start, HD)
            state = product_tn(split(k_ref[row, col]), split(v_ref[row, col]))
            if n > 0:
                state = state + before_ref[n - 1, head, :]
            if n + 1 < count:
                before_ref[n, head, :] = state
            else:
                total_ref[head, :] = state


def key_states_other(k_hbm, v_hbm, gain_hbm, total_ref, before_ref, k_ref, v_ref, gain_ref, sems, gain_sem):
    gain_copy = pltpu.make_async_copy(gain_hbm, gain_ref, gain_sem)
    copies = []
    for n, row in enumerate(blocks(k_ref.shape[0])):
        copies.append([
            pltpu.make_async_copy(far.at[row], near.at[row], sems.at[i, n])
            for i, (far, near) in enumerate(((k_hbm, k_ref), (v_hbm, v_ref)))
        ])
        for copy in copies[n]:
            copy.start()
    gain_copy.start()

    def ready(n):
        for copy in copies[n]:
            copy.wait()

    block_states(k_ref, v_ref, False, total_ref, before_ref, ready)
    gain_copy.wait()


def key_states_mine(k_ref, v_ref, q_ref, cot_ref, gain_ref, total_ref, before_ref, mine_ref, other_ref):
    half = k_ref.shape[1] // 2
    block_states(k_ref, v_ref, True, total_ref, before_ref)
    for mine, pack_ref in ((True, mine_ref), (False, other_ref)):
        col = half_cols(half, mine)
        pack_ref[:half, :] = q_ref[:, col].T
        pack_ref[half:, :] = (gain_ref[:, col] * cot_ref[:, col]).T


def state_times(state, query):
    left = split(state.T)
    twice = jnp.concatenate([query[0], query[0]], axis=0)
    return mul(beside(*left), twice, NN) + mul(left[0], query[1], NN)


def over_steps(left, right):
    rows, cols = left[0].shape[0], right[0].shape[0]
    wide = mul(jnp.concatenate(left, axis=0), jnp.concatenate(right, axis=0), NT)
    return wide[:rows, :cols] + wide[:rows, cols:] + wide[rows:, :cols]


def attend_local(pack_mine_ref, pack_other_ref, k_ref, v_ref, before_mine_ref, before_other_ref, mine_ref, other_ref):
    rows, width = k_ref.shape
    half = width // 2
    parts = ((False, pack_other_ref, before_other_ref, other_ref), (True, pack_mine_ref, before_mine_ref, mine_ref))
    for mine, pack_ref, before_ref, out_ref in parts:
        for head in heads(half):
            col = half_cols(half, mine, head.start, HD)
            for n, row in enumerate(blocks(rows)):
                query = split(pack_ref[head, row])
                key = split(k_ref[row, col])
                twice = jnp.concatenate([query[0], query[0]], axis=0)
                scores = mul(beside(*key), twice, NN) + mul(key[0], query[1], NN)
                scores = split(jnp.where(causal_mask(scores.shape[0], True), scores, 0.0))
                value = split(v_ref[row, col].T)
                out = mul(value[0], scores[0], NN) + mul(value[0], scores[1], NN) + mul(value[1], scores[0], NN)
                if n > 0:
                    out = out + state_times(before_ref[n - 1, head, :], query)
                out_ref[head, row] = out


def lane_rows(x):
    return [x[:, start : start + LANES] for start in range(0, x.shape[1], LANES)]


def attend_state(own_ref, own_local_ref, sib_ref, sib_local_ref, keep_ref, give_ref, own_out_ref, sib_out_ref, sums_ref):
    half, rows = own_local_ref.shape
    count = rows // LANES
    for core, pack_ref, local_ref, state_ref, out_ref in (
        (my_core(), own_ref, own_local_ref, keep_ref, own_out_ref),
        (1 - my_core(), sib_ref, sib_local_ref, give_ref, sib_out_ref),
    ):
        squares, cross = jnp.zeros((1, rows), F32), jnp.zeros((1, rows), F32)
        for head in heads(half):
            out = local_ref[head, :] + state_times(state_ref[head, :], split(pack_ref[head, :]))
            out_ref[head, :] = out
            scaled = pack_ref[half + head.start : half + head.stop, :]
            squares = squares + jnp.sum(out * out, axis=0, keepdims=True)
            cross = cross + jnp.sum(scaled * out, axis=0, keepdims=True)
        place = pl.ds(pl.multiple_of(core * 2 * count, 2 * count), 2 * count)
        sums_ref[place, :] = jnp.concatenate(lane_rows(squares) + lane_rows(cross), axis=0)


def attend_other(pair_sums_ref, got_ref, pack_ref, local_ref, out_ref, same_sums_ref):
    same_sums_ref[...] = pair_sums_ref[...]
    start = pair_sums_ref.shape[0]
    for head in heads(local_ref.shape[0]):
        state = got_ref[start + head.start : start + head.stop, :]
        out_ref[head, :] = local_ref[head, :] + state_times(state, split(pack_ref[head, :]))


def step_factors(full_width, rows, sums_ref, own):
    count = rows // LANES
    core = my_core() if own else 1 - my_core()
    sums = sums_ref[pl.ds(pl.multiple_of(core * 2 * count, 2 * count), 2 * count), :]
    inverse = lax.rsqrt(sums[:count] / full_width + 1e-06)
    factor = inverse * inverse * inverse * (sums[count:] / full_width)
    return [beside(*[x[j : j + 1, :] for j in range(count)]) for x in (inverse, factor)]


def gradient(factors, pack_ref, att_ref, head):
    half = att_ref.shape[0]
    scaled = pack_ref[half + head.start : half + head.stop, :]
    return split(factors[0] * scaled - factors[1] * att_ref[head, :])


def steps(parts, row):
    return [part[:, row] for part in parts]


def grad_states(full_width, sums_ref, own_ref, sib_ref, own_att_ref, sib_att_ref, pair_ref, own_total_ref, sib_total_ref, after_ref, high_ref, low_ref):
    half, rows = own_att_ref.shape
    for own, pack_ref, att_ref, total_ref in ((False, sib_ref, sib_att_ref, sib_total_ref), (True, own_ref, own_att_ref, own_total_ref)):
        factors = step_factors(full_width, rows, sums_ref, own)
        for head in heads(half):
            grad = gradient(factors, pack_ref, att_ref, head)
            query = split(pack_ref[head, :])
            total = None
            for n, row in reversed(list(enumerate(blocks(rows)))):
                state = over_steps(steps(grad, row), steps(query, row))
                total = state if total is None else total + state
                if own and n > 0:
                    after_ref[n - 1, head, :] = total
            if own:
                high_ref[head, :], low_ref[head, :] = grad
            total_ref[head, :] = total
    pair_ref[...] = own_total_ref[...] + sib_total_ref[...]


def grads_local(full_width, sums_ref, got_ref, high_ref, low_ref, att_other_ref, pack_mine_ref, pack_other_ref, k_ref, v_ref, keep_ref, before_mine_ref, before_other_ref, total_ref, gq_hbm, gk_ref, gv_ref, after_ref, same_total_ref, gq_ref, grad_high, grad_low, sems):
    rows, width = k_ref.shape
    half = width // 2
    sums_rows = 4 * rows // LANES
    same_total_ref[...] = total_ref[...]
    factors = step_factors(full_width, rows, sums_ref, True)
    copies = []
    for mine in (True, False):
        pack_ref, before_ref = (pack_mine_ref, before_mine_ref) if mine else (pack_other_ref, before_other_ref)
        for head in heads(half):
            col = half_cols(half, mine, head.start, HD)
            place = head if mine else slice(half + head.start, half + head.stop)
            if mine:
                state = keep_ref[head, :]
                grad = high_ref[head, :], low_ref[head, :]
            else:
                state = got_ref[sums_rows + head.start : sums_rows + head.stop, :]
                grad = gradient(factors, pack_ref, att_other_ref, head)
                query = split(pack_ref[head, :])
                total = None
            for n, row in reversed(list(enumerate(blocks(rows)))):
                part = steps(grad, row)
                if not mine and n > 0:
                    more = over_steps(part, steps(query, row))
                    total = more if total is None else total + more
                    after_ref[n - 1, head, :] = total
                part = [x.T for x in part]
                grad_high[row, place], grad_low[row, place] = part
                here = state_operand(state if n == 0 else state + before_ref[n - 1, head, :], True)
                gq_ref[row, col] = product_state(part, here, True)
    for mine in (True, False):
        for head in heads(half):
            col = half_cols(half, mine, head.start, HD)
            place = head if mine else slice(half + head.start, half + head.stop)
            for row in blocks(rows):
                grad = grad_high[row, place], grad_low[row, place]
                mixing = product_nt(grad, split(v_ref[row, col]))
                mixing = jnp.where(causal_mask(row.stop - row.start), mixing, 0.0)
                gq_ref[row, col] += product_nn(split(mixing), split(k_ref[row, col]))
                copies.append(pltpu.make_async_copy(gq_ref.at[row, col], gq_hbm.at[row, col], sems.at[len(copies)]))
                copies[-1].start()
    for mine in (True, False):
        pack_ref = pack_mine_ref if mine else pack_other_ref
        for head in heads(half):
            col = half_cols(half, mine, head.start, HD)
            place = head if mine else slice(half + head.start, half + head.stop)
            for row in blocks(rows):
                grad = grad_high[row, place], grad_low[row, place]
                query, key, value = split(pack_ref[head, row].T), split(k_ref[row, col]), split(v_ref[row, col])
                mask = causal_mask(row.stop - row.start, True)
                mixing = jnp.where(mask, product_nt(value, grad), 0.0)
                gk_ref[row, place] = product_nn(split(mixing), query)
                scores = jnp.where(mask, product_nt(key, query), 0.0)
                gv_ref[row, place] = product_nn(split(scores), grad)
    for copy in copies:
        copy.wait()


def grads_state(mine, k_ref, v_ref, gk_local_ref, gv_local_ref, state_ref, after_ref, *refs):
    gk_hbm, gv_hbm, gk_ref, gv_ref, sems = refs[-5:]
    rows, width = k_ref.shape
    half = width // 2
    last = len(blocks(rows)) - 1
    copies = []

    def leave(near, far, row, head, col):
        copies.append(pltpu.make_async_copy(near.at[row, head], far.at[row, col], sems.at[len(copies)]))
        copies[-1].start()

    for head in heads(half):
        col = half_cols(half, mine, head.start, HD)
        place = head if mine else slice(half + head.start, half + head.stop)
        states = [state_ref[head, :] if n == last else state_ref[head, :] + after_ref[n, head, :] for n in range(last + 1)]
        for here, row in zip(states, blocks(rows)):
            gk_ref[row, head] = gk_local_ref[row, place] + product_state(split(v_ref[row, col]), state_operand(here, False), False)
            leave(gk_ref, gk_hbm, row, head, col)
        for here, row in zip(states, blocks(rows)):
            gv_ref[row, head] = gv_local_ref[row, place] + product_state(split(k_ref[row, col]), state_operand(here, True), True)
            leave(gv_ref, gv_hbm, row, head, col)
    for copy in copies:
        copy.wait()


def swap(x, axis, distance):
    count = lax.axis_size(axis)
    return lax.ppermute(x, axis, [(i, i ^ distance) for i in range(count)])


def from_other_chips(pair, reverse):
    place = lax.axis_index("seq")
    chip = place // 2
    ahead = lambda d: (chip ^ d) > chip if reverse else (chip ^ d) < chip
    total = jnp.zeros_like(pair)
    if on_grid():
        got = [(d, swap(pair, "seq", 2 * d + d % 2)) for d in (3, 1, 2)]
        for d, part in got:
            total = total + jnp.where(ahead(d), part, 0.0)
        return total
    d = 1
    while d < lax.axis_size("seq") // 2:
        part = swap(pair, "seq", 2 * d)
        total = total + jnp.where(ahead(d), part, 0.0)
        pair = pair + part
        d *= 2
    return total


def sum_over_heads(x, same_x):
    count = lax.axis_size("head")
    if count > 4 or count & (count - 1):
        return lax.psum(same_x, "head")
    parts = []
    seqs = range(lax.axis_size("seq"))
    for d in sorted(range(1, count), key=lambda d: (d != count // 2, -d)):
        pairs = [(i * count + z, (i ^ 1) * count + (z ^ d)) for i in seqs for z in range(count)]
        parts.append(lax.ppermute(x, ("seq", "head"), pairs))
    for part in parts:
        same_x = same_x + part
    return same_x


def shards(queries, keys, values, cotangent, gain):
    rows, width = queries.shape
    full_width = width * lax.axis_size("head")
    half = width // 2
    count = len(blocks(rows))
    units = count * (width // HD)
    square = rows * width * HD * 2 * 3
    whole, halves, state = (rows, width), (rows, half), (half, HD)
    packed, across = (2 * half, rows), (half, rows)
    inner = (max(count - 1, 1), half, HD)
    first = lax.axis_index("seq") % 2 == 0
    gain = gain.reshape(1, width)

    other, before_other, near_keys, near_values, gain = call(
        key_states_other, "key_states_other", [state, inner, whole, whole, (1, width)], square // 2,
        [keys, values, gain], [pltpu.SemaphoreType.DMA((2, count)), pltpu.SemaphoreType.DMA], hbm_in=(0, 1, 2),
    )
    from_pair = swap(other, "seq", 1)
    mine, before_mine, pack_mine, pack_other = call(
        key_states_mine, "key_states_mine", [state, inner, packed, packed], square // 2,
        [near_keys, near_values, queries, cotangent, gain],
    )
    sibling = swap(pack_other, "seq", 1)
    earlier = from_other_chips(mine + from_pair, False)
    keep = earlier + jnp.where(first, 0.0, from_pair)
    give = earlier + jnp.where(first, mine, 0.0)
    local_mine, local_other = call(
        attend_local, "attend_local", [across, across], 5 * square,
        [pack_mine, pack_other, near_keys, near_values, before_mine, before_other],
    )
    sibling_local = swap(local_other, "seq", 1)
    attended, sibling_attended, sums = call(
        attend_state, "attend_state", [across, across, (4 * rows // LANES, LANES)], square,
        [pack_mine, local_mine, sibling, sibling_local, keep, give],
    )
    given = jnp.concatenate([sums, give], axis=0)
    got = swap(given, "seq", 1)
    pair_sums = given[: sums.shape[0]] + got[: sums.shape[0]]
    attended_other, same_pair_sums = call(
        attend_other, "attend_other", [across, sums.shape], square // 2, [pair_sums, got, pack_other, local_other]
    )
    sums = sum_over_heads(pair_sums, same_pair_sums)
    pair, own_grad, sibling_grad, after_mine, high, low = call(
        functools.partial(grad_states, full_width), "grad_states",
        [state, state, state, inner, (across, BF16), (across, BF16)], square,
        [sums, pack_mine, sibling, attended, sibling_attended],
    )
    later = from_other_chips(pair, True)
    grad_q, local_k, local_v, after_other, own_grad = call(
        functools.partial(grads_local, full_width), "grads_local", [whole, whole, whole, inner, state], 14 * square,
        [sums, got, high, low, attended_other, pack_mine, pack_other, keys, values, keep, before_mine, before_other, own_grad],
        [pltpu.VMEM(whole, F32), pltpu.VMEM(whole, BF16), pltpu.VMEM(whole, BF16), pltpu.SemaphoreType.DMA((units,))],
        hbm_out=(0,),
    )
    keep_later = later + jnp.where(first, sibling_grad, 0.0)
    got_later = swap(later + jnp.where(first, 0.0, own_grad), "seq", 1)
    scratch = [pltpu.VMEM(halves, F32), pltpu.VMEM(halves, F32), pltpu.SemaphoreType.DMA((units,))]
    grad_k, grad_v = call(
        functools.partial(grads_state, True), "grads_state_mine", [whole] * 2, square,
        [keys, values, local_k, local_v, keep_later, after_mine], scratch, hbm_out=(0, 1),
    )
    grad_k, grad_v = call(
        functools.partial(grads_state, False), "grads_state_other", [whole] * 2, square,
        [keys, values, local_k, local_v, got_later, after_other, grad_k, grad_v], scratch,
        hbm_in=(6, 7), hbm_out=(0, 1), aliases={6: 0, 7: 1},
    )
    return grad_q, grad_k, grad_v


def solution(mesh):
    in_specs = (P("seq", "head"), P("seq", "head"), P("seq", "head"), P("seq", "head"), P("head"))
    out_specs = (P("seq", "head"), P("seq", "head"), P("seq", "head"))
    return jax.shard_map(shards, mesh=mesh, in_specs=in_specs, out_specs=out_specs, check_vma=False)
```
